32 devices in a mesh: slab: 8 (over y, x, core), orb: 4 (over z).
Axes of the slice: x: 2, y: 2, z: 4, core: 2. Of those that a mesh axis runs over, the one named last changes fastest.
Arguments:
- orbitals: float32 [256, 64, 4096], P('orb', 'slab'), may hold values from -6 to 6
- pair_list: int32 [32, 2], P(('slab', 'orb')), may hold values from 0 to 255, as said below
- box_start: int32 [32, 3], P(('slab', 'orb')), may hold values from 0 to 63
Outputs:
- exchange_action: float32 [256, 64, 4096], P('orb', 'slab')
The draws below stay inside these ranges and needn't reach their ends.
Inputs may be any that keep to these rules, and one draw needn't show every extreme that they name: `pair_list`: the two orbitals of a row differ.
All inputs are finite; a program needn't handle non-finite values.
Results may differ from the reference program's by a relative error of at most 0.0003.
Values sent between devices are 32-bit elements; how exact they have to be, the bound alone decides.
No kernel may reach another device: no remote copies, remote signals or barrier semaphores. Data moves between devices by JAX's collectives and lax.ppermute only.
A program may use at most 192 MiB of HBM per device.

```python
import jax
import jax.numpy as jnp
from jax import lax

NX = 64
NY = 64
NZ = 64
ITERS = 16
NORB = 256
NPAIRS = 32


def draw_pair_list(key, part):
    orb_key, offset_key = jax.random.split(jax.random.fold_in(key, 17))
    first_orb = jax.random.randint(orb_key, (NPAIRS,), 0, NORB)
    offset = jax.random.randint(offset_key, (NPAIRS,), 1, NORB)
    return jnp.stack([first_orb, (first_orb + offset) % NORB], axis=1).astype(jnp.int32)


def with_ends(entries, rng, low, high):
    dims = entries.shape
    index_at = [jax.random.randint(jax.random.fold_in(rng, axis), (), 0, dims[axis]) for axis in range(len(dims))]
    entries = entries.at[tuple(index_at)].set(low)
    longest = dims.index(max(dims))
    index_at[longest] = (index_at[longest] + 1) % dims[longest]
    return entries.at[tuple(index_at)].set(high)


def level_of(key, extent, cuts, least, top_value):
    factor_of, own = 1.0, jax.random.fold_in(key, 6)
    for axis_at, parts in cuts:
        steps = jnp.exp(jax.random.uniform(jax.random.fold_in(own, axis_at), (parts,), jnp.float32, least / len(cuts), top_value / len(cuts)))
        factor_of = factor_of * jnp.repeat(steps, extent[axis_at] // parts).reshape([-1 if axis == axis_at else 1 for axis in range(len(extent))])
    return factor_of


def gaussian(own_key, shape, spread, limit, shards=(), held_as=jnp.bfloat16):
    level = level_of(own_key, shape, shards, -0.22, 0.18) if shards else 1.0
    entries = jax.random.normal(own_key, shape, jnp.float32) * spread * level
    return jnp.minimum(jnp.maximum(entries, -limit), limit).astype(held_as)


def setup_inputs(seed: int = 0) -> dict:
    splits = jax.random.split(jax.random.key(seed), 4)
    orbitals = gaussian(splits[0], (NORB, NX, NY * NZ), 1.0, 6.0, ((0, 4), (1, 8)), jnp.float32)
    pair_list = draw_pair_list(jax.random.fold_in(splits[3], 71), 0)
    box_start = with_ends(jax.random.randint(splits[2], (NPAIRS, 3), 0, NX), jax.random.fold_in(splits[2], 1), 0, NX - 1).astype(jnp.int32)
    return dict(orbitals=orbitals, pair_list=pair_list, box_start=box_start)


screening = 0.02
center_eig = 6.0 + screening
half_width = 6.0
sigma_one = center_eig / half_width


def operate(field):
    grid = field.reshape(NX, NY, NZ)
    beside = jnp.roll(grid, 1, 0) + jnp.roll(grid, -1, 0)
    beside = beside + jnp.roll(grid, 1, 1) + jnp.roll(grid, -1, 1)
    beside = beside + jnp.roll(grid, 1, 2) + jnp.roll(grid, -1, 2)
    return (center_eig * grid - beside).reshape(NX, NY * NZ)


def solve_screened(density):
    def sweep(step_index, state_now):
        solution, residue, update, ratio = state_now
        solution = solution + update
        residue = residue - operate(update)
        ratio_next = 1.0 / (2.0 * sigma_one - ratio)
        update = ratio_next * ratio * update + (2.0 * ratio_next / half_width) * residue
        return (solution, residue, update, ratio_next)

    start_state = (jnp.zeros_like(density), density, density / center_eig,
                   jnp.asarray(1.0 / sigma_one, jnp.float32))
    return lax.fori_loop(0, ITERS, sweep, start_state)[0]


def box_of(corner):
    x_index = jnp.arange(NX, dtype=jnp.int32)
    cell_index = jnp.arange(NY * NZ, dtype=jnp.int32)
    y_index = cell_index // NZ
    z_index = cell_index % NZ
    inside_x = ((x_index - corner[0]) % NX) < NX // 2
    inside_y = ((y_index - corner[1]) % NY) < NY // 2
    inside_z = ((z_index - corner[2]) % NZ) < NZ // 2
    return (inside_x[:, None] & (inside_y & inside_z)[None, :]).astype(jnp.float32)


def reference(orbitals, pair_list, box_start):
    def one_pair(action, inputs):
        pair_row, corner = inputs
        first_orb = pair_row[0]
        second_orb = pair_row[1]
        mask = box_of(corner)
        left = orbitals[first_orb] * mask
        right = orbitals[second_orb] * mask
        potential = solve_screened(left * right)
        action = action.at[first_orb].add(-potential * right)
        action = action.at[second_orb].add(-potential * left)
        return action, None

    action, unused = lax.scan(one_pair, jnp.zeros_like(orbitals), (pair_list, box_start))
    return action
```

```python
import functools

import jax
import jax.numpy as jnp
import numpy as np
from jax import lax
from jax.experimental import pallas as pl
from jax.experimental.pallas import tpu as pltpu
from jax.sharding import PartitionSpec as P

NY = 64
NZ = 64
ITERS = 16
HALF = 32
FULL = 64
PACKED = HALF * HALF
MODES = 48
MARGIN = (MODES - HALF) // 2
PERIOD = 2 * (MODES + 1)
LANES = 128
FIELDS = 8
VMEM_LIMIT = 56 * 1024 * 1024

screening = 0.02
center_eig = 6.0 + screening
half_width = 6.0
sigma_one = center_eig / half_width


def spectrum():
    cosine = np.cos(np.pi * (np.arange(MODES) + 1) / (MODES + 1))
    lam = center_eig - 2.0 * (
        cosine[:, None, None] + cosine[None, :, None] + cosine[None, None, :]
    )
    solution_now, residue, ratio = np.zeros_like(lam), np.ones_like(lam), 1.0 / sigma_one
    update = residue / center_eig
    for _ in range(ITERS):
        solution_now = solution_now + update
        residue = residue - lam * update
        ratio_next = 1.0 / (2.0 * sigma_one - ratio)
        update = ratio_next * ratio * update + 2.0 * ratio_next / half_width * residue
        ratio = ratio_next
    table = -solution_now * (2.0 / (MODES + 1)) ** 3
    table = np.pad(table, ((0, 0), (0, 0), (0, LANES // 2 - MODES)))
    table = table.reshape(MODES // 16, 2, 8, MODES, LANES // 2).transpose(3, 2, 0, 1, 4)
    return table.reshape(MODES * 8, MODES // 16 * LANES).astype(np.float32)


def sine(mode, cell, start):
    place = (cell - start) & (HALF - 1)
    phase = ((mode + 1) * (place + MARGIN + 1)) % PERIOD
    return jnp.sin(phase.astype(jnp.float32) * np.float32(np.pi / (MODES + 1)))


def split(full):
    high = full.astype(jnp.bfloat16)
    return high, (full - high.astype(jnp.float32)).astype(jnp.bfloat16)


def halves(full):
    high = lax.reduce_precision(full, 8, 7)
    return high.astype(jnp.bfloat16), (full - high).astype(jnp.bfloat16)


def iotas(shape):
    return [lax.broadcasted_iota(jnp.int32, shape, d) for d in range(len(shape))]


def cell_y(q, g):
    return 2 * q + (g >> 1) + HALF // 2 * (g & 1)


def matrices(box_start):
    count = box_start.shape[0]
    bx, by, bz = (box_start[:, d][:, None, None] for d in range(3))

    def x_of(k, r):
        return sine(k, r, bx)

    def y_of(row, col):
        g, q = col >> 6, (col >> 3) & 7
        return jnp.where((row & 7) == (col & 7), sine(row >> 3, cell_y(q, g), by), 0.0)

    def z_of(row, col):
        same = ((row >> 7) == ((col >> 6) & 1)) & (((row >> 5) & 3) == (col >> 7))
        kz = col & 63
        return jnp.where(same & (kz < MODES), sine(kz, row & 31, bz), 0.0)

    out = []
    for of, rows, cols in ((x_of, MODES, HALF), (z_of, 256, 512), (y_of, MODES * 8, 256)):
        _, row, col = iotas((count, rows, cols))
        out += halves(of(row, col))
        _, row, col = iotas((count, cols, rows))
        out += halves(of(col, row))
    return out


def lane(shape):
    return lax.broadcasted_iota(jnp.int32, shape, len(shape) - 1)


def in_box(cell, start):
    return ((cell - start) & (FULL - 1)) < HALF


def fold(full, start_y, start_z):
    rows = full.shape[0]
    at = lane((rows, LANES))
    upper = (at >> 6) & 1
    in_z = in_box(at & 31, start_z)
    first = (at & 63) < 32
    picked = []
    for v in range(HALF // 2):
        low = full[:, v * LANES : (v + 1) * LANES]
        high = full[:, (v + HALF // 2) * LANES : (v + HALF // 2 + 1) * LANES]
        picked.append(jnp.where(in_box(2 * v + upper, start_y), low, high))
    out = []
    for q in range(8):
        a, b = picked[q], picked[q + 8]
        a = jnp.where(in_z, a, pltpu.roll(a, 96, 1))
        b = jnp.where(in_z, pltpu.roll(b, 32, 1), b)
        out.append(jnp.where(first, a, b))
    return out


def unfold(packed, start_y, start_z, row_mask):
    rows = packed.shape[0]
    at = lane((rows, LANES))
    upper = (at >> 6) & 1
    inside = in_box(at & 63, start_z) & row_mask
    first = (at & 63) < 32
    out = [None] * 32
    for v in range(16):
        piece = packed[:, (v % 8) * LANES : (v % 8 + 1) * LANES]
        if v < 8:
            wide = jnp.where(first, piece, pltpu.roll(piece, 32, 1))
        else:
            wide = jnp.where(first, pltpu.roll(piece, 96, 1), piece)
        wide = jnp.where(inside, wide, 0.0)
        in_y = in_box(2 * v + upper, start_y)
        out[v] = jnp.where(in_y, wide, 0.0)
        out[v + 16] = jnp.where(in_y, 0.0, wide)
    return out


class Task:
    def __init__(self, table, place, g, pair_dev, orb_dev, slab_rows):
        row, off = g // pair_dev, (g % pair_dev) * FIELDS
        base = place[1] * orb_dev
        self.left = table[row, off] - base
        self.right = table[row, off + 1] - base
        self.x, self.y, self.z = (table[row, off + 2 + d] for d in range(3))
        first_row = place[0] * slab_rows
        self.first_row = first_row
        self.rows = slab_rows
        self.meets = in_box(first_row, self.x) | in_box(first_row + slab_rows - 1, self.x)
        self.has_left = (self.left >= 0) & (self.left < orb_dev)
        self.has_right = (self.right >= 0) & (self.right < orb_dev)

    def row_mask(self):
        at = lax.broadcasted_iota(jnp.int32, (self.rows, LANES), 0)
        return in_box(at + self.first_row, self.x)


def pack_kernel(pair_dev, table, place, orbitals, out, held, sems):
    orb_dev, slab_rows, _ = orbitals.shape
    pairs = out.shape[0]

    def task_of(g):
        return Task(table, place, g, pair_dev, orb_dev, slab_rows)

    def copy_of(index, slot):
        return pltpu.make_async_copy(orbitals.at[index], held.at[slot], sems.at[slot])

    @pl.loop(0, pairs)
    def _(g):
        t = task_of(g)

        @pl.when(t.has_left & t.meets)
        def _():
            copy_of(t.left, 2 * g).start()

        @pl.when(t.has_right & t.meets)
        def _():
            copy_of(t.right, 2 * g + 1).start()

    @pl.loop(0, pairs)
    def _(g):
        t = task_of(g)

        def put(full):
            mask = t.row_mask()
            for q, piece in enumerate(fold(full, t.y, t.z)):
                out[g, :, q * LANES : (q + 1) * LANES] = jnp.where(mask, piece, 0.0)

        @pl.when(t.has_left & t.meets)
        def _():
            copy_of(t.left, 2 * g).wait()

        @pl.when(t.has_right & t.meets)
        def _():
            copy_of(t.right, 2 * g + 1).wait()

        @pl.when(t.meets & t.has_left & t.has_right)
        def _():
            put(held[2 * g] * held[2 * g + 1])

        @pl.when(t.meets & (t.has_left != t.has_right))
        def _():
            put(held[2 * g + jnp.where(t.has_left, 0, 1)])

        @pl.when(jnp.logical_not(t.meets))
        def _():
            out[g] = jnp.zeros(out.shape[1:], jnp.float32)


def dot3(a, b):
    def dot(left, right):
        return jnp.dot(left, right, preferred_element_type=jnp.float32)

    return dot(a[0], b[0]) + (dot(a[0], b[1]) + dot(a[1], b[0]))


def tile(full, row, col):
    return full[row * 8 : row * 8 + 8, col * LANES : (col + 1) * LANES]


def blocks(rows):
    return jnp.concatenate([jnp.concatenate(r, axis=1) for r in rows], axis=0)


def potential_of(density, x, xt, z, zt, y, yt, weights):
    pairs_x = MODES // 16
    u = dot3(x, split(density))
    u = blocks(
        [[tile(u, 2 * tp + par, q) for par in range(2)] for tp in range(pairs_x) for q in range(8)]
    )
    u = dot3(split(u), z)
    u = blocks(
        [[tile(u, tp * 8 + q, g) for tp in range(pairs_x)] for g in range(4) for q in range(8)]
    )
    u = dot3(y, split(u)) * weights
    u = dot3(yt, split(u))
    u = blocks(
        [[tile(u, g * 8 + q, tp) for g in range(4)] for tp in range(pairs_x) for q in range(8)]
    )
    u = dot3(split(u), zt)
    u = blocks(
        [[tile(u, tp * 8 + q, par) for q in range(8)] for tp in range(pairs_x) for par in range(2)]
    )
    return dot3(xt, split(u))


def solve_kernel(orb_dev, own, received, *refs):
    mats, weights, out, held, back, sems = refs[:12], *refs[12:]
    pair_dev = received.shape[2]
    n_slab, rows = held.shape[1], held.shape[2]
    for i in range(pair_dev):
        plane = [own[i, side] // orb_dev for side in range(2)]
        ins = [
            pltpu.make_async_copy(received.at[:, plane[side], i], held.at[side], sems.at[side])
            for side in range(2)
        ]
        for c in ins:
            c.start()
        for c in ins:
            c.wait()
        half = n_slab // 2
        sides = [
            (held[side, :half] + held[side, half:]).reshape(HALF, PACKED) for side in range(2)
        ]
        together = plane[0] == plane[1]
        density = jnp.where(together, sides[0], sides[0] * sides[1])
        m = [(mats[k][i], mats[k + 1][i]) for k in range(0, 12, 2)]
        potential = potential_of(density, *m, weights[...])
        for side in range(2):
            term = jnp.where(together, potential, potential * sides[1 - side])
            term = term.reshape(half, rows, PACKED)
            back[side, :half] = term
            back[side, half:] = term
        outs = [
            pltpu.make_async_copy(back.at[side], out.at[:, plane[side], i], sems.at[side])
            for side in range(2)
        ]
        outs[0].start()

        @pl.when(jnp.logical_not(together))
        def _():
            outs[1].start()
            outs[1].wait()

        outs[0].wait()


def place_kernel(pair_dev, table, place, orbitals, returned, zeros, out, held, acc, flags, sems):
    del zeros
    orb_dev, slab_rows, _ = orbitals.shape
    pairs = returned.shape[0]

    def task_of(g):
        return Task(table, place, g, pair_dev, orb_dev, slab_rows)

    def both(t):
        return t.meets & t.has_left & t.has_right

    def copy_of(index, slot):
        return pltpu.make_async_copy(orbitals.at[index], held.at[slot], sems.at[slot])

    def copy_out(k):
        return pltpu.make_async_copy(acc.at[k], out.at[k], sems.at[2 * pairs + k])

    @pl.loop(0, orb_dev)
    def _(k):
        flags[k] = 0

    @pl.loop(0, pairs)
    def _(g):
        t = task_of(g)

        @pl.when(both(t))
        def _():
            copy_of(t.left, 2 * g).start()
            copy_of(t.right, 2 * g + 1).start()

    @pl.loop(0, pairs)
    def _(g):
        t = task_of(g)

        def add(k, factor_slot):
            pieces = unfold(returned[g], t.y, t.z, t.row_mask())

            def cols(v):
                return slice(v * LANES, (v + 1) * LANES)

            if factor_slot is not None:
                pieces = [p * held[factor_slot, :, cols(v)] for v, p in enumerate(pieces)]

            @pl.when(flags[k] == 0)
            def _():
                for v, p in enumerate(pieces):
                    acc[k, :, cols(v)] = p

            @pl.when(flags[k] != 0)
            def _():
                for v, p in enumerate(pieces):
                    acc[k, :, cols(v)] += p

            flags[k] = 1

        @pl.when(both(t))
        def _():
            copy_of(t.left, 2 * g).wait()
            copy_of(t.right, 2 * g + 1).wait()
            add(t.left, 2 * g + 1)
            add(t.right, 2 * g)

        @pl.when(t.meets & (t.has_left != t.has_right))
        def _():
            add(jnp.where(t.has_left, t.left, t.right), None)

    @pl.loop(0, orb_dev)
    def _(k):
        @pl.when(flags[k] != 0)
        def _():
            copy_out(k).start()

    @pl.loop(0, orb_dev)
    def _(k):
        @pl.when(flags[k] != 0)
        def _():
            copy_out(k).wait()


def body(orbitals, pair_list, box_start):
    n_slab = lax.axis_size("slab")
    n_orb = lax.axis_size("orb")
    axes = ("slab", "orb")
    orb_dev, slab_rows, cells = orbitals.shape
    pair_dev = pair_list.shape[0]
    devices = n_slab * n_orb
    pairs = devices * pair_dev
    place = jnp.stack([lax.axis_index("slab"), lax.axis_index("orb")]).astype(jnp.int32)

    smem = pl.BlockSpec(memory_space=pltpu.SMEM)
    vmem = pl.BlockSpec(memory_space=pltpu.VMEM)
    hbm = pl.BlockSpec(memory_space=pl.ANY)
    params = pltpu.CompilerParams(vmem_limit_bytes=VMEM_LIMIT)
    slots = (pairs, slab_rows, PACKED)

    own = jnp.pad(jnp.concatenate([pair_list, box_start], axis=1), ((0, 0), (0, FIELDS - 5)))
    row = own.reshape(1, pair_dev * FIELDS)
    row = jnp.pad(row, ((0, 0), (0, -row.shape[1] % LANES)))
    table = lax.all_to_all(
        jnp.broadcast_to(row, (devices, row.shape[1])), axes, split_axis=0, concat_axis=0, tiled=True
    )

    outgoing = pl.pallas_call(
        functools.partial(pack_kernel, pair_dev),
        out_shape=jax.ShapeDtypeStruct(slots, jnp.float32),
        in_specs=[smem, smem, hbm],
        out_specs=vmem,
        scratch_shapes=[
            pltpu.VMEM((2 * pairs, slab_rows, cells), jnp.float32),
            pltpu.SemaphoreType.DMA((2 * pairs,)),
        ],
        compiler_params=params,
        name="pack",
    )(table, place, orbitals)
    received = lax.all_to_all(outgoing, axes, split_axis=0, concat_axis=0, tiled=True)

    mats = matrices(box_start)
    solved = pl.pallas_call(
        functools.partial(solve_kernel, orb_dev),
        out_shape=jax.ShapeDtypeStruct((n_slab, n_orb, pair_dev, slab_rows, PACKED), jnp.float32),
        in_specs=[smem, hbm] + [vmem] * 13,
        out_specs=hbm,
        scratch_shapes=[
            pltpu.VMEM((2, n_slab, slab_rows, PACKED), jnp.float32),
            pltpu.VMEM((2, n_slab, slab_rows, PACKED), jnp.float32),
            pltpu.SemaphoreType.DMA((2,)),
        ],
        compiler_params=params,
        name="solve",
    )(
        pair_list,
        received.reshape(n_slab, n_orb, pair_dev, slab_rows, PACKED),
        *mats,
        jnp.asarray(spectrum()),
    )
    returned = lax.all_to_all(solved.reshape(slots), axes, split_axis=0, concat_axis=0, tiled=True)

    return pl.pallas_call(
        functools.partial(place_kernel, pair_dev),
        out_shape=jax.ShapeDtypeStruct(orbitals.shape, jnp.float32),
        in_specs=[smem, smem, hbm, vmem, hbm],
        out_specs=hbm,
        scratch_shapes=[
            pltpu.VMEM((2 * pairs, slab_rows, cells), jnp.float32),
            pltpu.VMEM(orbitals.shape, jnp.float32),
            pltpu.SMEM((orb_dev,), jnp.int32),
            pltpu.SemaphoreType.DMA((2 * pairs + orb_dev,)),
        ],
        input_output_aliases={4: 0},
        compiler_params=params,
        name="place",
    )(table, place, orbitals, returned, jnp.zeros(orbitals.shape, jnp.float32))


def solution(mesh):
    return jax.shard_map(
        body,
        mesh=mesh,
        in_specs=(P("orb", "slab", None), P(("slab", "orb"), None), P(("slab", "orb"), None)),
        out_specs=P("orb", "slab", None),
        check_vma=False,
    )
```

```python
import functools

import jax
import jax.numpy as jnp
import numpy as np
from jax import lax
from jax.experimental import pallas as pl
from jax.experimental.pallas import tpu as pltpu
from jax.sharding import PartitionSpec as P

NY = 64
NZ = 64
ITERS = 16
HALF = 32
FULL = 64
PACKED = HALF * HALF
MODES = 48
MARGIN = (MODES - HALF) // 2
PERIOD = 2 * (MODES + 1)
LANES = 128
FIELDS = 8
CLEARS = 16
MIB = 1024 * 1024
COUNT, ORB, PAIR, SLOT, SECOND, START_X, START_Y, START_Z, BLANK = range(9)

screening = 0.02
center_eig = 6.0 + screening
half_width = 6.0
sigma_one = center_eig / half_width


def spectrum():
    cosine = np.cos(np.pi * (np.arange(MODES) + 1) / (MODES + 1))
    lam = center_eig - 2.0 * (
        cosine[:, None, None] + cosine[None, :, None] + cosine[None, None, :]
    )
    solution_now, residue, ratio = np.zeros_like(lam), np.ones_like(lam), 1.0 / sigma_one
    update = residue / center_eig
    for _ in range(ITERS):
        solution_now = solution_now + update
        residue = residue - lam * update
        ratio_next = 1.0 / (2.0 * sigma_one - ratio)
        update = ratio_next * ratio * update + 2.0 * ratio_next / half_width * residue
        ratio = ratio_next
    table = -solution_now * (2.0 / (MODES + 1)) ** 3
    table = np.pad(table, ((0, 0), (0, 0), (0, LANES // 2 - MODES)))
    table = table.reshape(MODES // 16, 2, 8, MODES, LANES // 2).transpose(3, 2, 0, 1, 4)
    return table.reshape(MODES * 8, MODES // 16 * LANES).astype(np.float32)


def sine(mode, cell, start):
    place = (cell - start) & (HALF - 1)
    phase = ((mode + 1) * (place + MARGIN + 1)) % PERIOD
    return jnp.sin(phase.astype(jnp.float32) * np.float32(np.pi / (MODES + 1)))


def split(full):
    high = full.astype(jnp.bfloat16)
    return high, (full - high.astype(jnp.float32)).astype(jnp.bfloat16)


def halves(full):
    high = lax.reduce_precision(full, 8, 7)
    return high.astype(jnp.bfloat16), (full - high).astype(jnp.bfloat16)


def iotas(shape):
    return [lax.broadcasted_iota(jnp.int32, shape, d) for d in range(len(shape))]


def cell_y(q, g):
    return 2 * q + (g >> 1) + HALF // 2 * (g & 1)


def matrices(box_start):
    count = box_start.shape[0]
    bx, by, bz = (box_start[:, d][:, None, None] for d in range(3))

    def x_of(k, r):
        return sine(k, r, bx)

    def y_of(row, col):
        g, q = col >> 6, (col >> 3) & 7
        return jnp.where((row & 7) == (col & 7), sine(row >> 3, cell_y(q, g), by), 0.0)

    def z_of(row, col):
        same = ((row >> 7) == ((col >> 6) & 1)) & (((row >> 5) & 3) == (col >> 7))
        kz = col & 63
        return jnp.where(same & (kz < MODES), sine(kz, row & 31, bz), 0.0)

    out = []
    for of, rows, cols in ((x_of, MODES, HALF), (z_of, 256, 512), (y_of, MODES * 8, 256)):
        _, row, col = iotas((count, rows, cols))
        out += halves(of(row, col))
        _, row, col = iotas((count, cols, rows))
        out += halves(of(col, row))
    return out


def lane(shape):
    return lax.broadcasted_iota(jnp.int32, shape, len(shape) - 1)


def in_box(cell, start):
    return ((cell - start) & (FULL - 1)) < HALF


def fold(full, start_y, start_z):
    rows = full.shape[0]
    at = lane((rows, LANES))
    upper = (at >> 6) & 1
    in_z = in_box(at & 31, start_z)
    first = (at & 63) < 32
    picked = []
    for v in range(HALF // 2):
        low = full[:, v * LANES : (v + 1) * LANES]
        high = full[:, (v + HALF // 2) * LANES : (v + HALF // 2 + 1) * LANES]
        picked.append(jnp.where(in_box(2 * v + upper, start_y), low, high))
    out = []
    for q in range(8):
        a, b = picked[q], picked[q + 8]
        a = jnp.where(in_z, a, pltpu.roll(a, 96, 1))
        b = jnp.where(in_z, pltpu.roll(b, 32, 1), b)
        out.append(jnp.where(first, a, b))
    return out


def unfold(packed, start_y, start_z, row_mask):
    rows = packed.shape[0]
    at = lane((rows, LANES))
    upper = (at >> 6) & 1
    inside = in_box(at & 63, start_z) & row_mask
    first = (at & 63) < 32
    out = [None] * 32
    for v in range(16):
        piece = packed[:, (v % 8) * LANES : (v % 8 + 1) * LANES]
        if v < 8:
            wide = jnp.where(first, piece, pltpu.roll(piece, 32, 1))
        else:
            wide = jnp.where(first, pltpu.roll(piece, 96, 1), piece)
        wide = jnp.where(inside, wide, 0.0)
        in_y = in_box(2 * v + upper, start_y)
        out[v] = jnp.where(in_y, wide, 0.0)
        out[v + 16] = jnp.where(in_y, 0.0, wide)
    return out


class Task:
    def __init__(self, table, place, g, pair_dev, orb_dev, slab_rows):
        row, off = g // pair_dev, (g % pair_dev) * FIELDS
        base = place[1] * orb_dev
        self.left = table[row, off] - base
        self.right = table[row, off + 1] - base
        self.x, self.y, self.z = (table[row, off + 2 + d] for d in range(3))
        first_row = place[0] * slab_rows
        self.meets = in_box(first_row, self.x) | in_box(first_row + slab_rows - 1, self.x)
        self.has_left = (self.left >= 0) & (self.left < orb_dev)
        self.has_right = (self.right >= 0) & (self.right < orb_dev)


def row_mask(place, rows, start_x):
    at = lax.broadcasted_iota(jnp.int32, (rows, LANES), 0)
    return in_box(at + place[0] * rows, start_x)


def pack_kernel(pair_dev, table, place, orbitals, out, work, held, packed, slot_of, sems, out_sems):
    orb_dev, slab_rows, _ = orbitals.shape
    pairs = out.shape[0]
    packed[pairs] = jnp.zeros(packed.shape[1:], jnp.float32)

    def copy_of(index, slot):
        return pltpu.make_async_copy(orbitals.at[index], held.at[slot], sems.at[slot])

    def send(g, source):
        return pltpu.make_async_copy(packed.at[source], out.at[g], out_sems.at[g])

    @pl.loop(0, orb_dev)
    def _(k):
        slot_of[k] = -1

    def entry(k, orbs):
        seen = slot_of[k] >= 0
        slot = jnp.where(seen, slot_of[k], orbs)

        @pl.when(jnp.logical_not(seen))
        def _():
            slot_of[k] = orbs
            work[ORB, orbs] = k
            copy_of(k, orbs).start()

        return slot, jnp.where(seen, orbs, orbs + 1)

    def scan(g, carry):
        terms, orbs, blanks = carry
        t = Task(table, place, g, pair_dev, orb_dev, slab_rows)
        any_here = t.has_left | t.has_right
        live = t.meets & any_here

        def listed(_):
            both = t.has_left & t.has_right
            a, orbs_a = entry(jnp.where(t.has_left, t.left, t.right), orbs)
            work[PAIR, terms] = g
            work[SLOT, terms] = a
            work[SECOND, terms] = -1
            work[START_X, terms] = t.x
            work[START_Y, terms] = t.y
            work[START_Z, terms] = t.z

            def second(_):
                b, orbs_b = entry(t.right, orbs_a)
                work[SECOND, terms] = b
                return orbs_b

            return terms + 1, lax.cond(both, second, lambda _: orbs_a, 0)

        terms, orbs = lax.cond(live, listed, lambda _: (terms, orbs), 0)
        blank = any_here & jnp.logical_not(t.meets)

        @pl.when(blank)
        def _():
            send(g, pairs).start()
            work[BLANK, blanks] = g

        return terms, orbs, jnp.where(blank, blanks + 1, blanks)

    terms, orbs, blanks = lax.fori_loop(0, pairs, scan, (0, 0, 0))
    work[COUNT, 0] = terms
    work[COUNT, 1] = orbs

    @pl.loop(0, orbs)
    def _(e):
        copy_of(work[ORB, e], e).wait()

    @pl.loop(0, terms)
    def _(i):
        g, a, b = work[PAIR, i], work[SLOT, i], work[SECOND, i]

        def put(full):
            mask = row_mask(place, slab_rows, work[START_X, i])
            for q, piece in enumerate(fold(full, work[START_Y, i], work[START_Z, i])):
                packed[g, :, q * LANES : (q + 1) * LANES] = jnp.where(mask, piece, 0.0)
            send(g, g).start()

        @pl.when(b >= 0)
        def _():
            put(held[a] * held[b])

        @pl.when(b < 0)
        def _():
            put(held[a])

    @pl.loop(0, terms)
    def _(i):
        send(work[PAIR, i], work[PAIR, i]).wait()

    @pl.loop(0, blanks)
    def _(i):
        send(work[BLANK, i], pairs).wait()


def clear_kernel(work, out, done, blank, sems):
    done[...] = jnp.full(done.shape, work[COUNT, 0], jnp.int32)
    count = blank.shape[0]
    blank[...] = jnp.zeros(blank.shape, jnp.float32)
    copies = [
        pltpu.make_async_copy(blank, out.at[c * count : (c + 1) * count], sems.at[c])
        for c in range(CLEARS)
    ]
    for c in copies:
        c.start()
    for c in copies:
        c.wait()


def dot3(a, b):
    def dot(left, right):
        return jnp.dot(left, right, preferred_element_type=jnp.float32)

    return dot(a[0], b[0]) + (dot(a[0], b[1]) + dot(a[1], b[0]))


def tile(full, row, col):
    return full[row * 8 : row * 8 + 8, col * LANES : (col + 1) * LANES]


def blocks(rows):
    return jnp.concatenate([jnp.concatenate(r, axis=1) for r in rows], axis=0)


def potential_of(density, x, xt, z, zt, y, yt, weights):
    pairs_x = MODES // 16
    u = dot3(x, split(density))
    u = blocks(
        [[tile(u, 2 * tp + par, q) for par in range(2)] for tp in range(pairs_x) for q in range(8)]
    )
    u = dot3(split(u), z)
    u = blocks(
        [[tile(u, tp * 8 + q, g) for tp in range(pairs_x)] for g in range(4) for q in range(8)]
    )
    u = dot3(y, split(u)) * weights
    u = dot3(yt, split(u))
    u = blocks(
        [[tile(u, g * 8 + q, tp) for g in range(4)] for tp in range(pairs_x) for q in range(8)]
    )
    u = dot3(split(u), zt)
    u = blocks(
        [[tile(u, tp * 8 + q, par) for q in range(8)] for tp in range(pairs_x) for par in range(2)]
    )
    return dot3(xt, split(u))


def solve_kernel(orb_dev, own, received, cleared, *refs):
    del cleared
    mats, weights, out, held, back, sems = refs[:12], *refs[12:]
    pair_dev = received.shape[2]
    n_slab, rows = held.shape[1], held.shape[2]
    for i in range(pair_dev):
        plane = [own[i, side] // orb_dev for side in range(2)]
        ins = [
            pltpu.make_async_copy(received.at[:, plane[side], i], held.at[side], sems.at[side])
            for side in range(2)
        ]
        for c in ins:
            c.start()
        for c in ins:
            c.wait()
        half = n_slab // 2
        sides = [
            (held[side, :half] + held[side, half:]).reshape(HALF, PACKED) for side in range(2)
        ]
        together = plane[0] == plane[1]
        density = jnp.where(together, sides[0], sides[0] * sides[1])
        m = [(mats[k][i], mats[k + 1][i]) for k in range(0, 12, 2)]
        potential = potential_of(density, *m, weights[...])
        for side in range(2):
            term = jnp.where(together, potential, potential * sides[1 - side])
            term = term.reshape(half, rows, PACKED)
            back[side, :half] = term
            back[side, half:] = term
        outs = [
            pltpu.make_async_copy(back.at[side], out.at[:, plane[side], i], sems.at[side])
            for side in range(2)
        ]
        outs[0].start()

        @pl.when(jnp.logical_not(together))
        def _():
            outs[1].start()
            outs[1].wait()

        outs[0].wait()


def place_kernel(work, place, orbitals, returned, zeros, out, held, arrived, acc, sems, in_sems):
    del zeros
    _, slab_rows, _ = orbitals.shape
    terms, orbs = work[COUNT, 0], work[COUNT, 1]

    def copy_of(e):
        return pltpu.make_async_copy(orbitals.at[work[ORB, e]], held.at[e], sems.at[e])

    def copy_out(e):
        return pltpu.make_async_copy(acc.at[e], out.at[work[ORB, e]], sems.at[e])

    def take(i):
        g = work[PAIR, i]
        return pltpu.make_async_copy(returned.at[g], arrived.at[i], in_sems.at[i])

    @pl.loop(0, terms)
    def _(i):
        take(i).start()

        @pl.when(work[SECOND, i] >= 0)
        def _():
            pair = copy_of(work[SLOT, i]), copy_of(work[SECOND, i])
            for c in pair:
                c.start()
            for c in pair:
                c.wait()

    @pl.loop(0, orbs)
    def _(e):
        acc[e] = jnp.zeros(acc.shape[1:], jnp.float32)

    @pl.loop(0, terms)
    def _(i):
        a, b = work[SLOT, i], work[SECOND, i]
        take(i).wait()
        mask = row_mask(place, slab_rows, work[START_X, i])
        pieces = unfold(arrived[i], work[START_Y, i], work[START_Z, i], mask)

        @pl.when(b >= 0)
        def _():
            for v, p in enumerate(pieces):
                cols = slice(v * LANES, (v + 1) * LANES)
                acc[a, :, cols] += p * held[b, :, cols]
                acc[b, :, cols] += p * held[a, :, cols]

        @pl.when(b < 0)
        def _():
            for v, p in enumerate(pieces):
                acc[a, :, v * LANES : (v + 1) * LANES] += p

    @pl.loop(0, orbs)
    def _(e):
        copy_out(e).start()

    @pl.loop(0, orbs)
    def _(e):
        copy_out(e).wait()


def body(orbitals, pair_list, box_start):
    n_slab = lax.axis_size("slab")
    n_orb = lax.axis_size("orb")
    axes = ("slab", "orb")
    orb_dev, slab_rows, cells = orbitals.shape
    pair_dev = pair_list.shape[0]
    devices = n_slab * n_orb
    pairs = devices * pair_dev
    place = jnp.stack([lax.axis_index("slab"), lax.axis_index("orb")]).astype(jnp.int32)

    smem = pl.BlockSpec(memory_space=pltpu.SMEM)
    vmem = pl.BlockSpec(memory_space=pltpu.VMEM)
    free = pl.BlockSpec(memory_space=pl.ANY)
    hbm = pl.BlockSpec(memory_space=pltpu.HBM)
    slots = (pairs, slab_rows, PACKED)
    many = min(2 * pairs, orb_dev)
    held = pltpu.VMEM((many, slab_rows, cells), jnp.float32)

    def grant(mib):
        return pltpu.CompilerParams(vmem_limit_bytes=mib * MIB)

    own = jnp.pad(jnp.concatenate([pair_list, box_start], axis=1), ((0, 0), (0, FIELDS - 5)))
    row = own.reshape(1, pair_dev * FIELDS)
    row = jnp.pad(row, ((0, 0), (0, -row.shape[1] % LANES)))
    table = lax.all_to_all(
        jnp.broadcast_to(row, (devices, row.shape[1])), axes, split_axis=0, concat_axis=0, tiled=True
    )

    outgoing, work = pl.pallas_call(
        functools.partial(pack_kernel, pair_dev),
        out_shape=[
            jax.ShapeDtypeStruct(slots, jnp.float32),
            jax.ShapeDtypeStruct((9, max(many, pairs)), jnp.int32),
        ],
        in_specs=[smem, smem, hbm],
        out_specs=[free, smem],
        scratch_shapes=[
            held,
            pltpu.VMEM((pairs + 1, slab_rows, PACKED), jnp.float32),
            pltpu.SMEM((orb_dev,), jnp.int32),
            pltpu.SemaphoreType.DMA((many,)),
            pltpu.SemaphoreType.DMA((pairs,)),
        ],
        compiler_params=grant(56),
        name="pack",
    )(table, place, orbitals)
    received = lax.all_to_all(outgoing, axes, split_axis=0, concat_axis=0, tiled=True)

    zeros, cleared = pl.pallas_call(
        clear_kernel,
        out_shape=[
            jax.ShapeDtypeStruct(orbitals.shape, jnp.float32),
            jax.ShapeDtypeStruct((8, LANES), jnp.int32),
        ],
        in_specs=[smem],
        out_specs=[hbm, vmem],
        scratch_shapes=[
            pltpu.VMEM((orb_dev // CLEARS, slab_rows, cells), jnp.float32),
            pltpu.SemaphoreType.DMA((CLEARS,)),
        ],
        compiler_params=grant(16),
        cost_estimate=pl.CostEstimate(
            flops=0, bytes_accessed=orbitals.size * 4, transcendentals=0
        ),
        name="clear",
    )(work)
    solved = pl.pallas_call(
        functools.partial(solve_kernel, orb_dev),
        out_shape=jax.ShapeDtypeStruct((n_slab, n_orb, pair_dev, slab_rows, PACKED), jnp.float32),
        in_specs=[smem, free] + [vmem] * 14,
        out_specs=free,
        scratch_shapes=[
            pltpu.VMEM((2, n_slab, slab_rows, PACKED), jnp.float32),
            pltpu.VMEM((2, n_slab, slab_rows, PACKED), jnp.float32),
            pltpu.SemaphoreType.DMA((2,)),
        ],
        compiler_params=grant(16),
        name="solve",
    )(
        pair_list,
        received.reshape(n_slab, n_orb, pair_dev, slab_rows, PACKED),
        cleared,
        *matrices(box_start),
        jnp.asarray(spectrum()),
    )
    returned = lax.all_to_all(solved.reshape(slots), axes, split_axis=0, concat_axis=0, tiled=True)

    return pl.pallas_call(
        place_kernel,
        out_shape=jax.ShapeDtypeStruct(orbitals.shape, jnp.float32),
        in_specs=[smem, smem, hbm, free, hbm],
        out_specs=hbm,
        scratch_shapes=[
            held,
            pltpu.VMEM(slots, jnp.float32),
            held,
            pltpu.SemaphoreType.DMA((many,)),
            pltpu.SemaphoreType.DMA((pairs,)),
        ],
        input_output_aliases={4: 0},
        compiler_params=grant(56),
        name="place",
    )(work, place, orbitals, returned, zeros)


def solution(mesh):
    return jax.shard_map(
        body,
        mesh=mesh,
        in_specs=(P("orb", "slab", None), P(("slab", "orb"), None), P(("slab", "orb"), None)),
        out_specs=P("orb", "slab", None),
        check_vma=False,
    )
```

```python
import functools

import jax
import jax.numpy as jnp
import numpy as np
from jax import lax
from jax.experimental import pallas as pl
from jax.experimental.pallas import tpu as pltpu
from jax.sharding import PartitionSpec as P

NY = 64
NZ = 64
ITERS = 16
HALF = 32
FULL = 64
PACKED = HALF * HALF
MODES = 48
MARGIN = (MODES - HALF) // 2
PERIOD = 2 * (MODES + 1)
LANES = 128
FIELDS = 8
CLEARS = 16
MIB = 1024 * 1024
COUNT, PAIR, SLOT, SECOND, FIRST_A, FIRST_B, LAST_A, LAST_B, START_X, START_Y, START_Z, BLANK = range(12)

screening = 0.02
center_eig = 6.0 + screening
half_width = 6.0
sigma_one = center_eig / half_width


def spectrum():
    cosine = np.cos(np.pi * (np.arange(MODES) + 1) / (MODES + 1))
    lam = center_eig - 2.0 * (
        cosine[:, None, None] + cosine[None, :, None] + cosine[None, None, :]
    )
    solution_now, residue, ratio = np.zeros_like(lam), np.ones_like(lam), 1.0 / sigma_one
    update = residue / center_eig
    for _ in range(ITERS):
        solution_now = solution_now + update
        residue = residue - lam * update
        ratio_next = 1.0 / (2.0 * sigma_one - ratio)
        update = ratio_next * ratio * update + 2.0 * ratio_next / half_width * residue
        ratio = ratio_next
    table = -solution_now * (2.0 / (MODES + 1)) ** 3
    table = np.pad(table, ((0, 0), (0, 0), (0, LANES // 2 - MODES)))
    table = table.reshape(MODES // 16, 2, 8, MODES, LANES // 2).transpose(3, 2, 0, 1, 4)
    return table.reshape(MODES * 8, MODES // 16 * LANES).astype(np.float32)


def sine(mode, cell, start):
    place = (cell - start) & (HALF - 1)
    phase = ((mode + 1) * (place + MARGIN + 1)) % PERIOD
    return jnp.sin(phase.astype(jnp.float32) * np.float32(np.pi / (MODES + 1)))


def split(full):
    high = full.astype(jnp.bfloat16)
    return high, (full - high.astype(jnp.float32)).astype(jnp.bfloat16)


def halves(full):
    high = lax.reduce_precision(full, 8, 7)
    return high.astype(jnp.bfloat16), (full - high).astype(jnp.bfloat16)


def iotas(shape):
    return [lax.broadcasted_iota(jnp.int32, shape, d) for d in range(len(shape))]


def cell_y(q, g):
    return 2 * q + (g >> 1) + HALF // 2 * (g & 1)


def matrices(box_start):
    count = box_start.shape[0]
    bx, by, bz = (box_start[:, d][:, None, None] for d in range(3))

    def x_of(k, r):
        return sine(k, r, bx)

    def y_of(row, col):
        g, q = col >> 6, (col >> 3) & 7
        return jnp.where((row & 7) == (col & 7), sine(row >> 3, cell_y(q, g), by), 0.0)

    def z_of(row, col):
        same = ((row >> 7) == ((col >> 6) & 1)) & (((row >> 5) & 3) == (col >> 7))
        kz = col & 63
        return jnp.where(same & (kz < MODES), sine(kz, row & 31, bz), 0.0)

    out = []
    for of, rows, cols in ((x_of, MODES, HALF), (z_of, 256, 512), (y_of, MODES * 8, 256)):
        _, row, col = iotas((count, rows, cols))
        out += halves(of(row, col))
        _, row, col = iotas((count, cols, rows))
        out += halves(of(col, row))
    return out


def lane(shape):
    return lax.broadcasted_iota(jnp.int32, shape, len(shape) - 1)


def in_box(cell, start):
    return ((cell - start) & (FULL - 1)) < HALF


def fold(full, start_y, start_z):
    rows = full.shape[0]
    at = lane((rows, LANES))
    upper = (at >> 6) & 1
    in_z = in_box(at & 31, start_z)
    first = (at & 63) < 32
    picked = []
    for v in range(HALF // 2):
        low = full[:, v * LANES : (v + 1) * LANES]
        high = full[:, (v + HALF // 2) * LANES : (v + HALF // 2 + 1) * LANES]
        picked.append(jnp.where(in_box(2 * v + upper, start_y), low, high))
    out = []
    for q in range(8):
        a, b = picked[q], picked[q + 8]
        a = jnp.where(in_z, a, pltpu.roll(a, 96, 1))
        b = jnp.where(in_z, pltpu.roll(b, 32, 1), b)
        out.append(jnp.where(first, a, b))
    return out


def unfold(packed, start_y, start_z, row_mask):
    rows = packed.shape[0]
    at = lane((rows, LANES))
    upper = (at >> 6) & 1
    inside = in_box(at & 63, start_z) & row_mask
    first = (at & 63) < 32
    out = [None] * 32
    for v in range(16):
        piece = packed[:, (v % 8) * LANES : (v % 8 + 1) * LANES]
        if v < 8:
            wide = jnp.where(first, piece, pltpu.roll(piece, 32, 1))
        else:
            wide = jnp.where(first, pltpu.roll(piece, 96, 1), piece)
        wide = jnp.where(inside, wide, 0.0)
        in_y = in_box(2 * v + upper, start_y)
        out[v] = jnp.where(in_y, wide, 0.0)
        out[v + 16] = jnp.where(in_y, 0.0, wide)
    return out


def row_mask(first_row, rows, start_x):
    at = lax.broadcasted_iota(jnp.int32, (rows, LANES), 0)
    return in_box(at + first_row, start_x)


def pack_kernel(pair_dev, table_in, orbitals, out, work, table, held, packed, seen, sems, out_sems, table_sem):
    orb_dev, slab_rows, _ = orbitals.shape
    pairs = out.shape[0]
    base, first_row = lax.axis_index("orb") * orb_dev, lax.axis_index("slab") * slab_rows
    table_copy = pltpu.make_async_copy(table_in, table, table_sem)
    table_copy.start()
    packed[pairs] = jnp.zeros(packed.shape[1:], jnp.float32)
    for k in range(orb_dev + 1):
        seen[k] = 0
    table_copy.wait()

    def copy_of(index, slot):
        return pltpu.make_async_copy(orbitals.at[index], held.at[slot], sems.at[slot])

    def send(g, source):
        return pltpu.make_async_copy(packed.at[source], out.at[g], out_sems.at[g])

    def scan(g, carry):
        terms, blanks = carry
        row, off = g // pair_dev, (g % pair_dev) * FIELDS
        left, right = table[row, off] - base, table[row, off + 1] - base
        x = table[row, off + 2]
        meets = in_box(first_row, x) | in_box(first_row + slab_rows - 1, x)
        has_left = (left >= 0) & (left < orb_dev)
        has_right = (right >= 0) & (right < orb_dev)
        here = has_left | has_right
        live = here & meets
        both = has_left & has_right
        a = jnp.where(has_left, left, right)
        b = jnp.where(both, right, -1)
        work[PAIR, terms] = g
        work[SLOT, terms] = a
        work[SECOND, terms] = b
        work[START_X, terms] = x
        work[START_Y, terms] = table[row, off + 3]
        work[START_Z, terms] = table[row, off + 4]
        work[BLANK, blanks] = g

        @pl.when(live)
        def _():
            copy_of(a, 2 * terms).start()

            @pl.when(both)
            def _():
                copy_of(b, 2 * terms + 1).start()

        for which, k, used in ((FIRST_A, a, live), (FIRST_B, b, live & both)):
            k = jnp.where(used, k, orb_dev)
            old = seen[k]
            work[which, terms] = old
            seen[k] = 1
        terms = terms + jnp.where(live, 1, 0)
        return terms, blanks + jnp.where(here & jnp.logical_not(meets), 1, 0)

    zero = jnp.int32(0)
    terms, blanks = lax.fori_loop(0, pairs, scan, (zero, zero), unroll=4)
    work[COUNT, 0] = terms
    work[COUNT, 1] = first_row

    @pl.loop(0, blanks)
    def _(i):
        send(work[BLANK, i], pairs).start()

    @pl.loop(0, terms)
    def _(n):
        i = terms - 1 - n
        for which, source in ((LAST_B, SECOND), (LAST_A, SLOT)):
            k = work[source, i]
            k = jnp.where(k < 0, orb_dev, k)
            work[which, i] = seen[k]
            seen[k] = 0

    @pl.loop(0, terms)
    def _(i):
        g = work[PAIR, i]

        def put(full):
            mask = row_mask(first_row, slab_rows, work[START_X, i])
            for q, piece in enumerate(fold(full, work[START_Y, i], work[START_Z, i])):
                packed[g, :, q * LANES : (q + 1) * LANES] = jnp.where(mask, piece, 0.0)
            send(g, g).start()

        copy_of(work[SLOT, i], 2 * i).wait()

        @pl.when(work[SECOND, i] >= 0)
        def _():
            copy_of(work[SECOND, i], 2 * i + 1).wait()
            put(held[2 * i] * held[2 * i + 1])

        @pl.when(work[SECOND, i] < 0)
        def _():
            put(held[2 * i])

    @pl.loop(0, terms)
    def _(i):
        send(work[PAIR, i], work[PAIR, i]).wait()

    @pl.loop(0, blanks)
    def _(i):
        send(work[BLANK, i], pairs).wait()


def clear_kernel(work, out, done, blank, sems):
    done[...] = jnp.full(done.shape, work[COUNT, 0], jnp.int32)
    count = blank.shape[0]
    blank[...] = jnp.zeros(blank.shape, jnp.float32)
    copies = [
        pltpu.make_async_copy(blank, out.at[c * count : (c + 1) * count], sems.at[c])
        for c in range(CLEARS)
    ]
    for c in copies:
        c.start()
    for c in copies:
        c.wait()


def dot3(a, b):
    def dot(left, right):
        return jnp.dot(left, right, preferred_element_type=jnp.float32)

    return dot(a[0], b[0]) + (dot(a[0], b[1]) + dot(a[1], b[0]))


def tile(full, row, col):
    return full[row * 8 : row * 8 + 8, col * LANES : (col + 1) * LANES]


def blocks(rows):
    return jnp.concatenate([jnp.concatenate(r, axis=1) for r in rows], axis=0)


def potential_of(density, x, xt, z, zt, y, yt, weights):
    pairs_x = MODES // 16
    u = dot3(x, split(density))
    u = blocks(
        [[tile(u, 2 * tp + par, q) for par in range(2)] for tp in range(pairs_x) for q in range(8)]
    )
    u = dot3(split(u), z)
    u = blocks(
        [[tile(u, tp * 8 + q, g) for tp in range(pairs_x)] for g in range(4) for q in range(8)]
    )
    u = dot3(y, split(u)) * weights
    u = dot3(yt, split(u))
    u = blocks(
        [[tile(u, g * 8 + q, tp) for g in range(4)] for tp in range(pairs_x) for q in range(8)]
    )
    u = dot3(split(u), zt)
    u = blocks(
        [[tile(u, tp * 8 + q, par) for q in range(8)] for tp in range(pairs_x) for par in range(2)]
    )
    return dot3(xt, split(u))


def solve_kernel(orb_dev, own, received, cleared, *refs):
    del cleared
    mats, weights, out = refs[:12], *refs[12:]
    n_slab, _, pair_dev, rows, _ = received.shape
    half = n_slab // 2
    for i in range(pair_dev):
        plane = [own[i, side] // orb_dev for side in range(2)]
        sides = [
            jnp.concatenate(
                [received[s, at, i] + received[s + half, at, i] for s in range(half)], axis=0
            )
            for at in plane
        ]
        together = plane[0] == plane[1]
        density = jnp.where(together, sides[0], sides[0] * sides[1])
        m = [(mats[k][i], mats[k + 1][i]) for k in range(0, 12, 2)]
        potential = potential_of(density, *m, weights[...])
        for side in range(2):
            term = jnp.where(together, potential, potential * sides[1 - side])
            for s in range(half):
                part = term[s * rows : (s + 1) * rows]
                out[s, plane[side], i] = part
                out[s + half, plane[side], i] = part


def place_kernel(work, orbitals, returned, zeros, out, held, acc, sems, out_sems):
    del zeros
    _, slab_rows, _ = orbitals.shape
    terms, first_row = work[COUNT, 0], work[COUNT, 1]

    def factors(i):
        return [
            pltpu.make_async_copy(
                orbitals.at[work[which, i]], held.at[2 * i + n], sems.at[2 * i + n]
            )
            for n, which in enumerate((SLOT, SECOND))
        ]

    def copy_out(k):
        return pltpu.make_async_copy(acc.at[k], out.at[k], out_sems.at[k])

    @pl.loop(0, terms)
    def _(i):
        @pl.when(work[SECOND, i] >= 0)
        def _():
            for c in factors(i):
                c.start()

    @pl.loop(0, terms)
    def _(i):
        a, b = work[SLOT, i], work[SECOND, i]
        mask = row_mask(first_row, slab_rows, work[START_X, i])
        pieces = unfold(returned[work[PAIR, i]], work[START_Y, i], work[START_Z, i], mask)

        def add(k, later, last, slot):
            def term(v):
                if slot is None:
                    return pieces[v]
                return pieces[v] * held[slot, :, v * LANES : (v + 1) * LANES]

            @pl.when(later == 0)
            def _():
                for v in range(len(pieces)):
                    acc[k, :, v * LANES : (v + 1) * LANES] = term(v)

            @pl.when(later != 0)
            def _():
                for v in range(len(pieces)):
                    acc[k, :, v * LANES : (v + 1) * LANES] += term(v)

            @pl.when(last != 0)
            def _():
                copy_out(k).start()

        @pl.when(b >= 0)
        def _():
            for c in factors(i):
                c.wait()
            add(a, work[FIRST_A, i], work[LAST_A, i], 2 * i + 1)
            add(b, work[FIRST_B, i], work[LAST_B, i], 2 * i)

        @pl.when(b < 0)
        def _():
            add(a, work[FIRST_A, i], work[LAST_A, i], None)

    @pl.loop(0, terms)
    def _(i):
        @pl.when(work[LAST_A, i] != 0)
        def _():
            copy_out(work[SLOT, i]).wait()

        @pl.when((work[SECOND, i] >= 0) & (work[LAST_B, i] != 0))
        def _():
            copy_out(work[SECOND, i]).wait()


def body(orbitals, pair_list, box_start):
    n_slab = lax.axis_size("slab")
    n_orb = lax.axis_size("orb")
    axes = ("slab", "orb")
    orb_dev, slab_rows, cells = orbitals.shape
    pair_dev = pair_list.shape[0]
    devices = n_slab * n_orb
    pairs = devices * pair_dev

    smem = pl.BlockSpec(memory_space=pltpu.SMEM)
    vmem = pl.BlockSpec(memory_space=pltpu.VMEM)
    free = pl.BlockSpec(memory_space=pl.ANY)
    hbm = pl.BlockSpec(memory_space=pltpu.HBM)
    slots = (pairs, slab_rows, PACKED)
    held = pltpu.VMEM((2 * pairs, slab_rows, cells), jnp.float32)

    def grant(mib):
        return pltpu.CompilerParams(vmem_limit_bytes=mib * MIB)

    width = -(-pair_dev * FIELDS // LANES) * LANES
    row = jnp.concatenate([pair_list, box_start], axis=1)
    row = jnp.pad(row, ((0, 0), (0, FIELDS - row.shape[1]))).reshape(1, pair_dev * FIELDS)
    row = jnp.pad(row, ((0, 0), (0, width - row.shape[1])))
    table = lax.all_to_all(
        jnp.broadcast_to(row, (devices, width)), axes, split_axis=0, concat_axis=0, tiled=True
    )

    outgoing, work = pl.pallas_call(
        functools.partial(pack_kernel, pair_dev),
        out_shape=[
            jax.ShapeDtypeStruct(slots, jnp.float32),
            jax.ShapeDtypeStruct((12, -(-(2 * pairs + 1) // LANES) * LANES), jnp.int32),
        ],
        in_specs=[free, hbm],
        out_specs=[hbm, smem],
        scratch_shapes=[
            pltpu.SMEM((devices, width), jnp.int32),
            held,
            pltpu.VMEM((pairs + 1, slab_rows, PACKED), jnp.float32),
            pltpu.SMEM((orb_dev + 1,), jnp.int32),
            pltpu.SemaphoreType.DMA((2 * pairs,)),
            pltpu.SemaphoreType.DMA((pairs,)),
            pltpu.SemaphoreType.DMA,
        ],
        compiler_params=grant(56),
        name="pack",
    )(table, orbitals)
    received = lax.all_to_all(outgoing, axes, split_axis=0, concat_axis=0, tiled=True)

    zeros, cleared = pl.pallas_call(
        clear_kernel,
        out_shape=[
            jax.ShapeDtypeStruct(orbitals.shape, jnp.float32),
            jax.ShapeDtypeStruct((8, LANES), jnp.int32),
        ],
        in_specs=[smem],
        out_specs=[hbm, vmem],
        scratch_shapes=[
            pltpu.VMEM((orb_dev // CLEARS, slab_rows, cells), jnp.float32),
            pltpu.SemaphoreType.DMA((CLEARS,)),
        ],
        compiler_params=grant(16),
        cost_estimate=pl.CostEstimate(
            flops=0, bytes_accessed=orbitals.size * 4, transcendentals=0
        ),
        name="clear",
    )(work)

    solved = pl.pallas_call(
        functools.partial(solve_kernel, orb_dev),
        out_shape=jax.ShapeDtypeStruct((n_slab, n_orb, pair_dev, slab_rows, PACKED), jnp.float32),
        in_specs=[smem] + [vmem] * 15,
        out_specs=vmem,
        compiler_params=grant(16),
        name="solve",
    )(
        pair_list,
        received.reshape(n_slab, n_orb, pair_dev, slab_rows, PACKED),
        cleared,
        *matrices(box_start),
        jnp.asarray(spectrum()),
    )
    returned = lax.all_to_all(solved.reshape(slots), axes, split_axis=0, concat_axis=0, tiled=True)

    return pl.pallas_call(
        place_kernel,
        out_shape=jax.ShapeDtypeStruct(orbitals.shape, jnp.float32),
        in_specs=[smem, hbm, vmem, hbm],
        out_specs=hbm,
        scratch_shapes=[
            held,
            pltpu.VMEM(orbitals.shape, jnp.float32),
            pltpu.SemaphoreType.DMA((2 * pairs,)),
            pltpu.SemaphoreType.DMA((orb_dev,)),
        ],
        input_output_aliases={3: 0},
        compiler_params=grant(52),
        name="place",
    )(work, orbitals, returned, zeros)


def solution(mesh):
    return jax.shard_map(
        body,
        mesh=mesh,
        in_specs=(P("orb", "slab", None), P(("slab", "orb"), None), P(("slab", "orb"), None)),
        out_specs=P("orb", "slab", None),
        check_vma=False,
    )
```

```python
import functools

import jax
import jax.numpy as jnp
import numpy as np
from jax import lax
from jax.experimental import pallas as pl
from jax.experimental.pallas import tpu as pltpu
from jax.sharding import PartitionSpec as P

NY = 64
NZ = 64
ITERS = 16
HALF = 32
FULL = 64
PACKED = HALF * HALF
MODES = 48
MARGIN = (MODES - HALF) // 2
PERIOD = 2 * (MODES + 1)
LANES = 128
FIELDS = 8
CLEARS = 16
MIB = 1024 * 1024
COUNT, PAIR, SLOT, SECOND, FIRST_A, FIRST_B, LAST_A, LAST_B, START_X, START_Y, START_Z, BLANK = range(12)
OWN_A, OWN_B, OWN_MEETS, OWN_X, OWN_Y, OWN_Z = range(12, 18)
FULL_ROWS = 24
BIG = 1 << 20

screening = 0.02
center_eig = 6.0 + screening
half_width = 6.0
sigma_one = center_eig / half_width


def spectrum():
    cosine = np.cos(np.pi * (np.arange(MODES) + 1) / (MODES + 1))
    lam = center_eig - 2.0 * (
        cosine[:, None, None] + cosine[None, :, None] + cosine[None, None, :]
    )
    solution_now, residue, ratio = np.zeros_like(lam), np.ones_like(lam), 1.0 / sigma_one
    update = residue / center_eig
    for _ in range(ITERS):
        solution_now = solution_now + update
        residue = residue - lam * update
        ratio_next = 1.0 / (2.0 * sigma_one - ratio)
        update = ratio_next * ratio * update + 2.0 * ratio_next / half_width * residue
        ratio = ratio_next
    table = -solution_now * (2.0 / (MODES + 1)) ** 3
    table = np.pad(table, ((0, 0), (0, 0), (0, LANES // 2 - MODES)))
    table = table.reshape(MODES // 16, 2, 8, MODES, LANES // 2).transpose(3, 2, 0, 1, 4)
    return table.reshape(MODES * 8, MODES // 16 * LANES).astype(np.float32)


def sine(mode, cell, start):
    place = (cell - start) & (HALF - 1)
    phase = ((mode + 1) * (place + MARGIN + 1)) % PERIOD
    return jnp.sin(phase.astype(jnp.float32) * np.float32(np.pi / (MODES + 1)))


def split(full):
    high = full.astype(jnp.bfloat16)
    return high, (full - high.astype(jnp.float32)).astype(jnp.bfloat16)


def halves(full):
    high = lax.reduce_precision(full, 8, 7)
    return high.astype(jnp.bfloat16), (full - high).astype(jnp.bfloat16)


def iotas(shape):
    return [lax.broadcasted_iota(jnp.int32, shape, d) for d in range(len(shape))]


def cell_y(q, g):
    return 2 * q + (g >> 1) + HALF // 2 * (g & 1)


def matrices(box_start):
    count = box_start.shape[0]
    bx, by, bz = (box_start[:, d][:, None, None] for d in range(3))

    def x_of(k, r):
        return sine(k, r, bx)

    def y_of(row, col):
        g, q = col >> 6, (col >> 3) & 7
        return jnp.where((row & 7) == (col & 7), sine(row >> 3, cell_y(q, g), by), 0.0)

    def z_of(row, col):
        same = ((row >> 7) == ((col >> 6) & 1)) & (((row >> 5) & 3) == (col >> 7))
        kz = col & 63
        return jnp.where(same & (kz < MODES), sine(kz, row & 31, bz), 0.0)

    out = []
    for of, rows, cols in ((x_of, MODES, HALF), (z_of, 256, 512), (y_of, MODES * 8, 256)):
        _, row, col = iotas((count, rows, cols))
        out += halves(of(row, col))
        _, row, col = iotas((count, cols, rows))
        out += halves(of(col, row))
    return out


def lane(shape):
    return lax.broadcasted_iota(jnp.int32, shape, len(shape) - 1)


def in_box(cell, start):
    return ((cell - start) & (FULL - 1)) < HALF


def fold(full, start_y, start_z):
    rows = full.shape[0]
    at = lane((rows, LANES))
    upper = (at >> 6) & 1
    in_z = in_box(at & 31, start_z)
    first = (at & 63) < 32
    picked = []
    for v in range(HALF // 2):
        low = full[:, v * LANES : (v + 1) * LANES]
        high = full[:, (v + HALF // 2) * LANES : (v + HALF // 2 + 1) * LANES]
        picked.append(jnp.where(in_box(2 * v + upper, start_y), low, high))
    out = []
    for q in range(8):
        a, b = picked[q], picked[q + 8]
        a = jnp.where(in_z, a, pltpu.roll(a, 96, 1))
        b = jnp.where(in_z, pltpu.roll(b, 32, 1), b)
        out.append(jnp.where(first, a, b))
    return out


def unfold(packed, start_y, start_z, row_mask):
    rows = packed.shape[0]
    at = lane((rows, LANES))
    upper = (at >> 6) & 1
    inside = in_box(at & 63, start_z) & row_mask
    first = (at & 63) < 32
    out = [None] * 32
    for v in range(16):
        piece = packed[:, (v % 8) * LANES : (v % 8 + 1) * LANES]
        if v < 8:
            wide = jnp.where(first, piece, pltpu.roll(piece, 32, 1))
        else:
            wide = jnp.where(first, pltpu.roll(piece, 96, 1), piece)
        wide = jnp.where(inside, wide, 0.0)
        in_y = in_box(2 * v + upper, start_y)
        out[v] = jnp.where(in_y, wide, 0.0)
        out[v + 16] = jnp.where(in_y, 0.0, wide)
    return out


def row_mask(first_row, rows, start_x):
    at = lax.broadcasted_iota(jnp.int32, (rows, LANES), 0)
    return in_box(at + first_row, start_x)


def mark_last(work, seen, terms, orb_dev):
    @pl.loop(0, terms)
    def _(n):
        i = terms - 1 - n
        for which, source in ((LAST_B, SECOND), (LAST_A, SLOT)):
            k = work[source, i]
            k = jnp.where(k < 0, orb_dev, k)
            work[which, i] = seen[k]
            seen[k] = 0


def pack_kernel(pair_dev, table_in, orbitals, out, work, table, held, packed, seen, sems, out_sems, table_sem):
    orb_dev, slab_rows, _ = orbitals.shape
    pairs = out.shape[0]
    base, first_row = lax.axis_index("orb") * orb_dev, lax.axis_index("slab") * slab_rows
    table_copy = pltpu.make_async_copy(table_in, table, table_sem)
    table_copy.start()
    packed[pairs] = jnp.zeros(packed.shape[1:], jnp.float32)
    for k in range(orb_dev + 1):
        seen[k] = 0
    table_copy.wait()

    def copy_of(index, slot):
        return pltpu.make_async_copy(orbitals.at[index], held.at[slot], sems.at[slot])

    def send(g, source):
        return pltpu.make_async_copy(packed.at[source], out.at[g], out_sems.at[g])

    def scan(g, carry):
        terms, blanks = carry
        row, off = g // pair_dev, (g % pair_dev) * FIELDS
        left, right = table[row, off] - base, table[row, off + 1] - base
        x = table[row, off + 2]
        meets = in_box(first_row, x) | in_box(first_row + slab_rows - 1, x)
        has_left = (left >= 0) & (left < orb_dev)
        has_right = (right >= 0) & (right < orb_dev)
        here = has_left | has_right
        live = here & meets
        both = has_left & has_right
        a = jnp.where(has_left, left, right)
        b = jnp.where(both, right, -1)
        work[PAIR, terms] = g
        work[SLOT, terms] = a
        work[SECOND, terms] = b
        work[START_X, terms] = x
        work[START_Y, terms] = table[row, off + 3]
        work[START_Z, terms] = table[row, off + 4]
        work[BLANK, blanks] = g

        @pl.when(live)
        def _():
            copy_of(a, 2 * terms).start()

            @pl.when(both)
            def _():
                copy_of(b, 2 * terms + 1).start()

        for which, k, used in ((FIRST_A, a, live), (FIRST_B, b, live & both)):
            k = jnp.where(used, k, orb_dev)
            old = seen[k]
            work[which, terms] = old
            seen[k] = 1
        terms = terms + jnp.where(live, 1, 0)
        return terms, blanks + jnp.where(here & jnp.logical_not(meets), 1, 0)

    zero = jnp.int32(0)
    terms, blanks = lax.fori_loop(0, pairs, scan, (zero, zero), unroll=4)
    work[COUNT, 0] = terms
    work[COUNT, 1] = first_row

    @pl.loop(0, blanks)
    def _(i):
        send(work[BLANK, i], pairs).start()

    mark_last(work, seen, terms, orb_dev)

    @pl.loop(0, terms)
    def _(i):
        g = work[PAIR, i]

        def put(full):
            mask = row_mask(first_row, slab_rows, work[START_X, i])
            for q, piece in enumerate(fold(full, work[START_Y, i], work[START_Z, i])):
                packed[g, :, q * LANES : (q + 1) * LANES] = jnp.where(mask, piece, 0.0)
            send(g, g).start()

        copy_of(work[SLOT, i], 2 * i).wait()

        @pl.when(work[SECOND, i] >= 0)
        def _():
            copy_of(work[SECOND, i], 2 * i + 1).wait()
            put(held[2 * i] * held[2 * i + 1])

        @pl.when(work[SECOND, i] < 0)
        def _():
            put(held[2 * i])

    @pl.loop(0, terms)
    def _(i):
        send(work[PAIR, i], work[PAIR, i]).wait()

    @pl.loop(0, blanks)
    def _(i):
        send(work[BLANK, i], pairs).wait()


def clear_kernel(work, out, done, blank, sems):
    done[...] = jnp.full(done.shape, work[COUNT, 0], jnp.int32)
    count = blank.shape[0]
    blank[...] = jnp.zeros(blank.shape, jnp.float32)
    copies = [
        pltpu.make_async_copy(blank, out.at[c * count : (c + 1) * count], sems.at[c])
        for c in range(CLEARS)
    ]
    for c in copies:
        c.start()
    for c in copies:
        c.wait()


def dot3(a, b):
    def dot(left, right):
        return jnp.dot(left, right, preferred_element_type=jnp.float32)

    return dot(a[0], b[0]) + (dot(a[0], b[1]) + dot(a[1], b[0]))


def tile(full, row, col):
    return full[row * 8 : row * 8 + 8, col * LANES : (col + 1) * LANES]


def blocks(rows):
    return jnp.concatenate([jnp.concatenate(r, axis=1) for r in rows], axis=0)


def potential_of(density, x, xt, z, zt, y, yt, weights):
    pairs_x = MODES // 16
    u = dot3(x, split(density))
    u = blocks(
        [[tile(u, 2 * tp + par, q) for par in range(2)] for tp in range(pairs_x) for q in range(8)]
    )
    u = dot3(split(u), z)
    u = blocks(
        [[tile(u, tp * 8 + q, g) for tp in range(pairs_x)] for g in range(4) for q in range(8)]
    )
    u = dot3(y, split(u)) * weights
    u = dot3(yt, split(u))
    u = blocks(
        [[tile(u, g * 8 + q, tp) for g in range(4)] for tp in range(pairs_x) for q in range(8)]
    )
    u = dot3(split(u), zt)
    u = blocks(
        [[tile(u, tp * 8 + q, par) for q in range(8)] for tp in range(pairs_x) for par in range(2)]
    )
    return dot3(xt, split(u))


def solve_kernel(orb_dev, own, received, cleared, *refs):
    del cleared
    mats, weights, out = refs[:12], *refs[12:]
    n_slab, _, pair_dev, rows, _ = received.shape
    half = n_slab // 2
    for i in range(pair_dev):
        plane = [own[i, side] // orb_dev for side in range(2)]
        sides = [
            jnp.concatenate(
                [received[s, at, i] + received[s + half, at, i] for s in range(half)], axis=0
            )
            for at in plane
        ]
        together = plane[0] == plane[1]
        density = jnp.where(together, sides[0], sides[0] * sides[1])
        m = [(mats[k][i], mats[k + 1][i]) for k in range(0, 12, 2)]
        potential = potential_of(density, *m, weights[...])
        for side in range(2):
            term = jnp.where(together, potential, potential * sides[1 - side])
            for s in range(half):
                part = term[s * rows : (s + 1) * rows]
                out[s, plane[side], i] = part
                out[s + half, plane[side], i] = part


def place_kernel(work, orbitals, returned, zeros, out, held, acc, sems, out_sems):
    del zeros
    place_terms(work, orbitals, lambda at: returned[at], out, held, acc, sems, out_sems)


def place_terms(work, orbitals, fetch, out, held, acc, sems, out_sems):
    _, slab_rows, _ = orbitals.shape
    terms, first_row = work[COUNT, 0], work[COUNT, 1]

    def factors(i):
        return [
            pltpu.make_async_copy(
                orbitals.at[work[which, i]], held.at[2 * i + n], sems.at[2 * i + n]
            )
            for n, which in enumerate((SLOT, SECOND))
        ]

    def copy_out(k):
        return pltpu.make_async_copy(acc.at[k], out.at[k], out_sems.at[k])

    @pl.loop(0, terms)
    def _(i):
        @pl.when(work[SECOND, i] >= 0)
        def _():
            for c in factors(i):
                c.start()

    @pl.loop(0, terms)
    def _(i):
        a, b = work[SLOT, i], work[SECOND, i]
        mask = row_mask(first_row, slab_rows, work[START_X, i])
        pieces = unfold(fetch(work[PAIR, i]), work[START_Y, i], work[START_Z, i], mask)

        def add(k, later, last, slot):
            def term(v):
                if slot is None:
                    return pieces[v]
                return pieces[v] * held[slot, :, v * LANES : (v + 1) * LANES]

            @pl.when(later == 0)
            def _():
                for v in range(len(pieces)):
                    acc[k, :, v * LANES : (v + 1) * LANES] = term(v)

            @pl.when(later != 0)
            def _():
                for v in range(len(pieces)):
                    acc[k, :, v * LANES : (v + 1) * LANES] += term(v)

            @pl.when(last != 0)
            def _():
                copy_out(k).start()

        @pl.when(b >= 0)
        def _():
            for c in factors(i):
                c.wait()
            add(a, work[FIRST_A, i], work[LAST_A, i], 2 * i + 1)
            add(b, work[FIRST_B, i], work[LAST_B, i], 2 * i)

        @pl.when(b < 0)
        def _():
            add(a, work[FIRST_A, i], work[LAST_A, i], None)

    @pl.loop(0, terms)
    def _(i):
        @pl.when(work[LAST_A, i] != 0)
        def _():
            copy_out(work[SLOT, i]).wait()

        @pl.when((work[SECOND, i] >= 0) & (work[LAST_B, i] != 0))
        def _():
            copy_out(work[SECOND, i]).wait()


def quotient(value, by):
    return value >> (by.bit_length() - 1) if by & (by - 1) == 0 else value // by


def pick(parts, index, act):
    begin = 0
    for part in parts:
        inside = (index >= begin) & (index < begin + part.shape[0])
        pl.when(inside)(lambda part=part, begin=begin: act(part, index - begin))
        begin += part.shape[0]


def slab_fields(n_slab, slab_rows):
    if n_slab > 8:
        return np.ones((FULL,), np.int32), 0
    bits = np.zeros((FULL,), np.int64)
    for x in range(FULL):
        for slab in range(n_slab):
            ends = (slab * slab_rows, (slab + 1) * slab_rows - 1)
            if any((e - x) % FULL < HALF for e in ends):
                bits[x] += 1 << (4 * slab)
    return bits.astype(np.uint32).view(np.int32), 4


def crossing_slots(cap, n_orb):
    return [max(cap * 3 // 4 if d == 1 else cap // 2, 1) for d in range(1, n_orb)]


def route_kernel(
    pair_dev, n_orb, width, table_in, fields, orbitals, *refs
):
    *sends, own, work, table, held, seen, load, pieces, crossing, chosen, sems, table_sem = refs
    orb_dev, slab_rows, _ = orbitals.shape
    pairs = table.shape[0] * pair_dev
    cap = own.shape[0]
    slots = crossing_slots(cap, n_orb)
    me = lax.axis_index("orb")
    slab = lax.axis_index("slab")
    base, first_row = me * orb_dev, slab * slab_rows
    table_copy = pltpu.make_async_copy(table_in, table, table_sem)
    table_copy.start()
    for k in range(orb_dev + 1):
        seen[k] = 0
    for k in range(n_orb):
        load[k] = 0
    for k in range(n_orb * n_orb):
        pieces[k] = 0
        crossing[k] = 0
    table_copy.wait()

    def copy_of(index, slot):
        return pltpu.make_async_copy(orbitals.at[index], held.at[slot], sems.at[slot])

    def scan(g, terms):
        row, off = g // pair_dev, (g % pair_dev) * FIELDS
        left, right = table[row, off], table[row, off + 1]
        x, y, z = (table[row, off + 2 + d] for d in range(3))
        a, b = quotient(left, orb_dev), quotient(right, orb_dev)
        weight = jnp.where((a ^ b) == 1, 0, 2)
        load_a, load_b = load[a], load[b]
        cost_a = jnp.where(load_a < cap, load_a + weight * pieces[b * n_orb + a], BIG)
        cost_b = jnp.where(load_b < cap, load_b + weight * pieces[a * n_orb + b], BIG)
        chosen[0] = jnp.where(cost_a <= cost_b, a, b)

        @pl.when((load_a >= cap) & (load_b >= cap))
        def _():
            least = jnp.int32(0)
            for o in range(1, n_orb):
                least = jnp.where(load[o] < load[least], o, least)
            chosen[0] = least

        k = chosen[0]
        j = load[k]
        load[k] = j + 1
        here = fields[x]
        meets = in_box(first_row, x) | in_box(first_row + slab_rows - 1, x)

        def cross(o, used):
            at = o * n_orb + k
            taken = crossing[at]
            crossing[at] = taken + jnp.where(used, here, 0)
            pieces[at] = pieces[at] + jnp.where(used, 1, 0)
            count = (taken >> (width * slab)) & 15 if width else taken
            d = o ^ k
            begin, room = jnp.int32(cap), jnp.int32(slots[0])
            for n in range(1, len(slots)):
                begin = jnp.where(d == n + 1, cap + sum(slots[:n]), begin)
                room = jnp.where(d == n + 1, slots[n], room)
            return begin + jnp.minimum(count, room - 1)

        away_a = a != k
        away_b = (b != k) & (a != b)
        at_a = cross(a, away_a)
        at_b = cross(b, away_b)
        mine = k == me

        @pl.when(mine)
        def _():
            both_away = away_a & away_b
            work[OWN_A, j] = jnp.where(both_away | (away_a & (a == b)), at_a, j)
            work[OWN_B, j] = jnp.where(away_b, at_b, jnp.where(away_a & (a != b), at_a, -1))
            work[OWN_MEETS, j] = jnp.where(meets, 1, 0)
            work[OWN_X, j] = x
            work[OWN_Y, j] = y
            work[OWN_Z, j] = z

        has_left, has_right = a == me, b == me
        live = (has_left | has_right) & meets
        both = has_left & has_right
        first = jnp.where(has_left, left, right) - base
        second = jnp.where(both, right - base, -1)
        work[PAIR, terms] = jnp.where(mine, j, jnp.where(has_left, at_a, at_b))
        work[SLOT, terms] = first
        work[SECOND, terms] = second
        work[START_X, terms] = x
        work[START_Y, terms] = y
        work[START_Z, terms] = z

        @pl.when(live)
        def _():
            copy_of(first, 2 * terms).start()

            @pl.when(both)
            def _():
                copy_of(second, 2 * terms + 1).start()

        for which, index, used in ((FIRST_A, first, live), (FIRST_B, second, live & both)):
            index = jnp.where(used, index, orb_dev)
            work[which, terms] = seen[index]
            seen[index] = 1
        return terms + jnp.where(live, 1, 0)

    terms = lax.fori_loop(0, pairs, scan, jnp.int32(0), unroll=2)
    over = jnp.int32(0)
    for o in range(n_orb):
        for k in range(n_orb):
            if o != k:
                room, count = slots[(o ^ k) - 1], crossing[o * n_orb + k]
                for f in range(8 if width else 1):
                    held_here = (count >> (width * f)) & 15 if width else count
                    over = over | jnp.where(held_here > room, 1, 0)
    work[COUNT, 0] = terms
    work[COUNT, 1] = first_row
    work[COUNT, 2] = over
    mark_last(work, seen, terms, orb_dev)

    @pl.loop(0, terms)
    def _(i):
        def put(full):
            mask = row_mask(first_row, slab_rows, work[START_X, i])
            folded = [
                jnp.where(mask, piece, 0.0)
                for piece in fold(full, work[START_Y, i], work[START_Z, i])
            ]

            def store(ref, n):
                for q, piece in enumerate(folded):
                    ref[n, :, q * LANES : (q + 1) * LANES] = piece

            pick([own, *sends], work[PAIR, i], store)

        copy_of(work[SLOT, i], 2 * i).wait()

        @pl.when(work[SECOND, i] >= 0)
        def _():
            copy_of(work[SECOND, i], 2 * i + 1).wait()
            put(held[2 * i] * held[2 * i + 1])

        @pl.when(work[SECOND, i] < 0)
        def _():
            put(held[2 * i])


def density_kernel(work, *refs):
    *parts, out, side = refs

    def load(ref, n):
        side[...] = ref[n]

    @pl.loop(0, out.shape[0])
    def _(j):
        a, b = work[OWN_A, j], work[OWN_B, j]
        meets = work[OWN_MEETS, j] != 0

        @pl.when(meets)
        def _():
            pick(parts, a, load)

        def both(ref, n):
            out[j] = side[...] * ref[n]

        @pl.when(meets & (b >= 0))
        def _():
            pick(parts, b, both)

        @pl.when(meets & (b < 0))
        def _():
            out[j] = side[...]

        @pl.when(jnp.logical_not(meets))
        def _():
            out[j] = jnp.zeros(out.shape[1:], jnp.float32)


def plane_solve_kernel(received, cleared, *refs):
    del cleared
    mats, weights, out = refs[:12], *refs[12:]
    n_slab, pair_dev, rows, _ = received.shape
    half = n_slab // 2
    for i in range(pair_dev):
        density = jnp.concatenate(
            [received[s, i] + received[s + half, i] for s in range(half)], axis=0
        )
        m = [(mats[k][i], mats[k + 1][i]) for k in range(0, 12, 2)]
        potential = potential_of(density, *m, weights[...])
        for s in range(half):
            part = potential[s * rows : (s + 1) * rows]
            out[s, i] = part
            out[s + half, i] = part


def term_kernel(work, potential, *refs):
    count = (len(refs) - 1) // 2
    parts, outs, term = refs[:count], refs[count : 2 * count], refs[-1]

    def store(ref, n):
        ref[n] = term[...]

    @pl.loop(0, potential.shape[0])
    def _(j):
        a, b = work[OWN_A, j], work[OWN_B, j]
        meets = work[OWN_MEETS, j] != 0

        def times(ref, n):
            term[...] = potential[j] * ref[n]

        @pl.when(meets & (b >= 0))
        def _():
            for source, target in ((a, b), (b, a)):
                pick(parts, source, times)
                pick(outs, target, store)

        @pl.when(meets & (b < 0))
        def _():
            term[...] = potential[j]
            pick(outs, a, store)


def plane_place_kernel(work, orbitals, zeros, *refs):
    del zeros
    *parts, out, held, acc, term, sems, out_sems = refs

    def load(ref, n):
        term[...] = ref[n]

    def fetch(at):
        pick(parts, at, load)
        return term[...]

    place_terms(work, orbitals, fetch, out, held, acc, sems, out_sems)


def body(orbitals, pair_list, box_start):
    n_slab = lax.axis_size("slab")
    n_orb = lax.axis_size("orb")
    axes = ("slab", "orb")
    orb_dev, slab_rows, cells = orbitals.shape
    pair_dev = pair_list.shape[0]
    devices = n_slab * n_orb
    pairs = devices * pair_dev

    smem = pl.BlockSpec(memory_space=pltpu.SMEM)
    vmem = pl.BlockSpec(memory_space=pltpu.VMEM)
    free = pl.BlockSpec(memory_space=pl.ANY)
    hbm = pl.BlockSpec(memory_space=pltpu.HBM)
    slots = (pairs, slab_rows, PACKED)
    held = pltpu.VMEM((2 * pairs, slab_rows, cells), jnp.float32)

    def grant(mib):
        return pltpu.CompilerParams(vmem_limit_bytes=mib * MIB)

    width = -(-pair_dev * FIELDS // LANES) * LANES
    row = jnp.concatenate([pair_list, box_start], axis=1)
    row = jnp.pad(row, ((0, 0), (0, FIELDS - row.shape[1]))).reshape(1, pair_dev * FIELDS)
    row = jnp.pad(row, ((0, 0), (0, width - row.shape[1])))
    table = lax.all_to_all(
        jnp.broadcast_to(row, (devices, width)), axes, split_axis=0, concat_axis=0, tiled=True
    )

    cap = pairs // n_orb
    crossings = crossing_slots(cap, n_orb)
    fields, field_bits = slab_fields(n_slab, slab_rows)
    lists = jax.ShapeDtypeStruct((FULL_ROWS, -(-(2 * pairs + 1) // LANES) * LANES), jnp.int32)
    one_plane = jax.ShapeDtypeStruct((cap, slab_rows, PACKED), jnp.float32)
    crossed = [jax.ShapeDtypeStruct((n, slab_rows, PACKED), jnp.float32) for n in crossings]
    one_slot = pltpu.VMEM((slab_rows, PACKED), jnp.float32)

    def cross(parts):
        return [
            lax.ppermute(part, "orb", [(o, o ^ (n + 1)) for o in range(n_orb)])
            for n, part in reversed(list(enumerate(parts)))
        ][::-1]

    def clear(work):
        return pl.pallas_call(
            clear_kernel,
            out_shape=[
                jax.ShapeDtypeStruct(orbitals.shape, jnp.float32),
                jax.ShapeDtypeStruct((8, LANES), jnp.int32),
            ],
            in_specs=[smem],
            out_specs=[hbm, vmem],
            scratch_shapes=[
                pltpu.VMEM((orb_dev // CLEARS, slab_rows, cells), jnp.float32),
                pltpu.SemaphoreType.DMA((CLEARS,)),
            ],
            compiler_params=grant(16),
            cost_estimate=pl.CostEstimate(
                flops=0, bytes_accessed=orbitals.size * 4, transcendentals=0
            ),
            name="clear",
        )(work)

    *sends, own_pieces, work = pl.pallas_call(
        functools.partial(route_kernel, pair_dev, n_orb, field_bits),
        out_shape=[*crossed, one_plane, lists],
        in_specs=[free, smem, hbm],
        out_specs=[vmem] * n_orb + [smem],
        scratch_shapes=[
            pltpu.SMEM((devices, width), jnp.int32),
            held,
            pltpu.SMEM((orb_dev + 1,), jnp.int32),
            pltpu.SMEM((n_orb,), jnp.int32),
            pltpu.SMEM((n_orb * n_orb,), jnp.int32),
            pltpu.SMEM((n_orb * n_orb,), jnp.int32),
            pltpu.SMEM((1,), jnp.int32),
            pltpu.SemaphoreType.DMA((2 * pairs,)),
            pltpu.SemaphoreType.DMA,
        ],
        compiler_params=grant(56),
        name="route",
    )(table, jnp.asarray(fields), orbitals)

    def in_planes(table, orbitals, box_start, work, own_pieces, *sends):
        del table, box_start
        arrived = cross(sends)
        zeros, cleared = clear(work)
        starts = lax.dynamic_slice(
            work, (OWN_X, lax.axis_index("slab") * pair_dev), (3, pair_dev)
        ).T
        mats = matrices(starts)
        density = pl.pallas_call(
            density_kernel,
            out_shape=one_plane,
            in_specs=[smem] + [vmem] * n_orb,
            out_specs=vmem,
            scratch_shapes=[one_slot],
            compiler_params=grant(8),
            name="density",
        )(work, own_pieces, *arrived)
        received = lax.all_to_all(density, "slab", split_axis=0, concat_axis=0, tiled=True)
        by_slab = (n_slab, pair_dev, slab_rows, PACKED)
        solved = pl.pallas_call(
            plane_solve_kernel,
            out_shape=jax.ShapeDtypeStruct(by_slab, jnp.float32),
            in_specs=[vmem] * 15,
            out_specs=vmem,
            compiler_params=grant(16),
            name="solve",
        )(received.reshape(by_slab), cleared, *mats, jnp.asarray(spectrum()))
        potential = lax.all_to_all(
            solved.reshape(one_plane.shape), "slab", split_axis=0, concat_axis=0, tiled=True
        )
        own_terms, *sends = pl.pallas_call(
            term_kernel,
            out_shape=[one_plane, *crossed],
            in_specs=[smem, vmem] + [vmem] * n_orb,
            out_specs=[vmem] * n_orb,
            scratch_shapes=[one_slot],
            compiler_params=grant(8),
            name="terms",
        )(work, potential, own_pieces, *arrived)
        arrived = cross(sends)
        return pl.pallas_call(
            plane_place_kernel,
            out_shape=jax.ShapeDtypeStruct(orbitals.shape, jnp.float32),
            in_specs=[smem, hbm, hbm] + [vmem] * n_orb,
            out_specs=hbm,
            scratch_shapes=[
                held,
                pltpu.VMEM(orbitals.shape, jnp.float32),
                one_slot,
                pltpu.SemaphoreType.DMA((2 * pairs,)),
                pltpu.SemaphoreType.DMA((orb_dev,)),
            ],
            input_output_aliases={2: 0},
            compiler_params=grant(52),
            name="place",
        )(work, orbitals, zeros, own_terms, *arrived)

    def direct(table, orbitals, box_start, *unused):
        del unused
        outgoing, work = pl.pallas_call(
            functools.partial(pack_kernel, pair_dev),
            out_shape=[
                jax.ShapeDtypeStruct(slots, jnp.float32),
                lists,
            ],
            in_specs=[free, hbm],
            out_specs=[hbm, smem],
            scratch_shapes=[
                pltpu.SMEM((devices, width), jnp.int32),
                held,
                pltpu.VMEM((pairs + 1, slab_rows, PACKED), jnp.float32),
                pltpu.SMEM((orb_dev + 1,), jnp.int32),
                pltpu.SemaphoreType.DMA((2 * pairs,)),
                pltpu.SemaphoreType.DMA((pairs,)),
                pltpu.SemaphoreType.DMA,
            ],
            compiler_params=grant(56),
            name="pack",
        )(table, orbitals)
        received = lax.all_to_all(outgoing, axes, split_axis=0, concat_axis=0, tiled=True)

        zeros, cleared = clear(work)

        solved = pl.pallas_call(
            functools.partial(solve_kernel, orb_dev),
            out_shape=jax.ShapeDtypeStruct((n_slab, n_orb, pair_dev, slab_rows, PACKED), jnp.float32),
            in_specs=[smem] + [vmem] * 15,
            out_specs=vmem,
            compiler_params=grant(16),
            name="solve",
        )(
            pair_list,
            received.reshape(n_slab, n_orb, pair_dev, slab_rows, PACKED),
            cleared,
            *matrices(box_start),
            jnp.asarray(spectrum()),
        )
        returned = lax.all_to_all(solved.reshape(slots), axes, split_axis=0, concat_axis=0, tiled=True)

        return pl.pallas_call(
            place_kernel,
            out_shape=jax.ShapeDtypeStruct(orbitals.shape, jnp.float32),
            in_specs=[smem, hbm, vmem, hbm],
            out_specs=hbm,
            scratch_shapes=[
                held,
                pltpu.VMEM(orbitals.shape, jnp.float32),
                pltpu.SemaphoreType.DMA((2 * pairs,)),
                pltpu.SemaphoreType.DMA((orb_dev,)),
            ],
            input_output_aliases={3: 0},
            compiler_params=grant(52),
            name="place",
        )(work, orbitals, returned, zeros)

    return lax.cond(
        work[COUNT, 2] > 0,
        direct,
        in_planes,
        table,
        orbitals,
        box_start,
        work,
        own_pieces,
        *sends,
    )


def solution(mesh):
    return jax.shard_map(
        body,
        mesh=mesh,
        in_specs=(P("orb", "slab", None), P(("slab", "orb"), None), P(("slab", "orb"), None)),
        out_specs=P("orb", "slab", None),
        check_vma=False,
    )
```

```python
import functools

import jax
import jax.numpy as jnp
import numpy as np
from jax import lax
from jax.experimental import pallas as pl
from jax.experimental.pallas import tpu as pltpu
from jax.sharding import PartitionSpec as P

NY = 64
NZ = 64
ITERS = 16
HALF = 32
FULL = 64
PACKED = HALF * HALF
MODES = 48
MARGIN = (MODES - HALF) // 2
PERIOD = 2 * (MODES + 1)
LANES = 128
FIELDS = 8
CLEARS = 16
MIB = 1024 * 1024
COUNT, PAIR, SLOT, SECOND, FIRST_A, FIRST_B, LAST_A, LAST_B, START_X, START_Y, START_Z, BLANK = range(12)
OWN_A, OWN_B, OWN_MEETS, OWN_X, OWN_Y, OWN_Z = range(12, 18)
FULL_ROWS = 24
BIG = 1 << 20

screening = 0.02
center_eig = 6.0 + screening
half_width = 6.0
sigma_one = center_eig / half_width


def spectrum():
    cosine = np.cos(np.pi * (np.arange(MODES) + 1) / (MODES + 1))
    lam = center_eig - 2.0 * (
        cosine[:, None, None] + cosine[None, :, None] + cosine[None, None, :]
    )
    solution_now, residue, ratio = np.zeros_like(lam), np.ones_like(lam), 1.0 / sigma_one
    update = residue / center_eig
    for _ in range(ITERS):
        solution_now = solution_now + update
        residue = residue - lam * update
        ratio_next = 1.0 / (2.0 * sigma_one - ratio)
        update = ratio_next * ratio * update + 2.0 * ratio_next / half_width * residue
        ratio = ratio_next
    table = -solution_now * (2.0 / (MODES + 1)) ** 3
    table = np.pad(table, ((0, 0), (0, 0), (0, LANES // 2 - MODES)))
    table = table.reshape(MODES // 16, 2, 8, MODES, LANES // 2).transpose(3, 2, 0, 1, 4)
    return table.reshape(MODES * 8, MODES // 16 * LANES).astype(np.float32)


def sine(mode, cell, start):
    place = (cell - start) & (HALF - 1)
    phase = ((mode + 1) * (place + MARGIN + 1)) % PERIOD
    return jnp.sin(phase.astype(jnp.float32) * np.float32(np.pi / (MODES + 1)))


def split(full):
    high = full.astype(jnp.bfloat16)
    return high, (full - high.astype(jnp.float32)).astype(jnp.bfloat16)


def halves(full):
    high = lax.reduce_precision(full, 8, 7)
    return high.astype(jnp.bfloat16), (full - high).astype(jnp.bfloat16)


def iotas(shape):
    return [lax.broadcasted_iota(jnp.int32, shape, d) for d in range(len(shape))]


def cell_y(q, g):
    return 2 * q + (g >> 1) + HALF // 2 * (g & 1)


def matrices(*starts):
    count = starts[0].shape[0]
    bx, by, bz = (start[:, None, None] for start in starts)

    def x_of(k, r):
        return sine(k, r, bx)

    def y_of(row, col):
        g, q = col >> 6, (col >> 3) & 7
        return jnp.where((row & 7) == (col & 7), sine(row >> 3, cell_y(q, g), by), 0.0)

    def z_of(row, col):
        same = ((row >> 7) == ((col >> 6) & 1)) & (((row >> 5) & 3) == (col >> 7))
        kz = col & 63
        return jnp.where(same & (kz < MODES), sine(kz, row & 31, bz), 0.0)

    out = []
    for of, rows, cols in ((x_of, MODES, HALF), (z_of, 256, 512), (y_of, MODES * 8, 256)):
        _, row, col = iotas((count, rows, cols))
        out += halves(of(row, col))
        _, row, col = iotas((count, cols, rows))
        out += halves(of(col, row))
    return out


def lane(shape):
    return lax.broadcasted_iota(jnp.int32, shape, len(shape) - 1)


def in_box(cell, start):
    return ((cell - start) & (FULL - 1)) < HALF


def fold(full, start_y, start_z):
    rows = full.shape[0]
    at = lane((rows, LANES))
    upper = (at >> 6) & 1
    in_z = in_box(at & 31, start_z)
    first = (at & 63) < 32
    picked = []
    for v in range(HALF // 2):
        low = full[:, v * LANES : (v + 1) * LANES]
        high = full[:, (v + HALF // 2) * LANES : (v + HALF // 2 + 1) * LANES]
        picked.append(jnp.where(in_box(2 * v + upper, start_y), low, high))
    out = []
    for q in range(8):
        a, b = picked[q], picked[q + 8]
        a = jnp.where(in_z, a, pltpu.roll(a, 96, 1))
        b = jnp.where(in_z, pltpu.roll(b, 32, 1), b)
        out.append(jnp.where(first, a, b))
    return out


def unfold(packed, start_y, start_z, row_mask):
    rows = packed.shape[0]
    at = lane((rows, LANES))
    upper = (at >> 6) & 1
    inside = in_box(at & 63, start_z) & row_mask
    first = (at & 63) < 32
    out = [None] * 32
    for v in range(16):
        piece = packed[:, (v % 8) * LANES : (v % 8 + 1) * LANES]
        if v < 8:
            wide = jnp.where(first, piece, pltpu.roll(piece, 32, 1))
        else:
            wide = jnp.where(first, pltpu.roll(piece, 96, 1), piece)
        wide = jnp.where(inside, wide, 0.0)
        in_y = in_box(2 * v + upper, start_y)
        out[v] = jnp.where(in_y, wide, 0.0)
        out[v + 16] = jnp.where(in_y, 0.0, wide)
    return out


def row_mask(first_row, rows, start_x):
    at = lax.broadcasted_iota(jnp.int32, (rows, LANES), 0)
    return in_box(at + first_row, start_x)


def mark_last(work, seen, terms, orb_dev):
    @pl.loop(0, terms)
    def _(n):
        i = terms - 1 - n
        for which, source in ((LAST_B, SECOND), (LAST_A, SLOT)):
            k = work[source, i]
            k = jnp.where(k < 0, orb_dev, k)
            work[which, i] = seen[k]
            seen[k] = 0


def pack_kernel(pair_dev, table_in, orbitals, out, work, table, held, packed, seen, sems, out_sems, table_sem):
    orb_dev, slab_rows, _ = orbitals.shape
    pairs = out.shape[0]
    base, first_row = lax.axis_index("orb") * orb_dev, lax.axis_index("slab") * slab_rows
    table_copy = pltpu.make_async_copy(table_in, table, table_sem)
    table_copy.start()
    packed[pairs] = jnp.zeros(packed.shape[1:], jnp.float32)
    for k in range(orb_dev + 1):
        seen[k] = 0
    table_copy.wait()

    def copy_of(index, slot):
        return pltpu.make_async_copy(orbitals.at[index], held.at[slot], sems.at[slot])

    def send(g, source):
        return pltpu.make_async_copy(packed.at[source], out.at[g], out_sems.at[g])

    def scan(g, carry):
        terms, blanks = carry
        row, off = g // pair_dev, (g % pair_dev) * FIELDS
        left, right = table[row, off] - base, table[row, off + 1] - base
        x = table[row, off + 2]
        meets = in_box(first_row, x) | in_box(first_row + slab_rows - 1, x)
        has_left = (left >= 0) & (left < orb_dev)
        has_right = (right >= 0) & (right < orb_dev)
        here = has_left | has_right
        live = here & meets
        both = has_left & has_right
        a = jnp.where(has_left, left, right)
        b = jnp.where(both, right, -1)
        work[PAIR, terms] = g
        work[SLOT, terms] = a
        work[SECOND, terms] = b
        work[START_X, terms] = x
        work[START_Y, terms] = table[row, off + 3]
        work[START_Z, terms] = table[row, off + 4]
        work[BLANK, blanks] = g

        @pl.when(live)
        def _():
            copy_of(a, 2 * terms).start()

            @pl.when(both)
            def _():
                copy_of(b, 2 * terms + 1).start()

        for which, k, used in ((FIRST_A, a, live), (FIRST_B, b, live & both)):
            k = jnp.where(used, k, orb_dev)
            old = seen[k]
            work[which, terms] = old
            seen[k] = 1
        terms = terms + jnp.where(live, 1, 0)
        return terms, blanks + jnp.where(here & jnp.logical_not(meets), 1, 0)

    zero = jnp.int32(0)
    terms, blanks = lax.fori_loop(0, pairs, scan, (zero, zero), unroll=4)
    work[COUNT, 0] = terms
    work[COUNT, 1] = first_row

    @pl.loop(0, blanks)
    def _(i):
        send(work[BLANK, i], pairs).start()

    mark_last(work, seen, terms, orb_dev)

    @pl.loop(0, terms)
    def _(i):
        g = work[PAIR, i]

        def put(full):
            mask = row_mask(first_row, slab_rows, work[START_X, i])
            for q, piece in enumerate(fold(full, work[START_Y, i], work[START_Z, i])):
                packed[g, :, q * LANES : (q + 1) * LANES] = jnp.where(mask, piece, 0.0)
            send(g, g).start()

        copy_of(work[SLOT, i], 2 * i).wait()

        @pl.when(work[SECOND, i] >= 0)
        def _():
            copy_of(work[SECOND, i], 2 * i + 1).wait()
            put(held[2 * i] * held[2 * i + 1])

        @pl.when(work[SECOND, i] < 0)
        def _():
            put(held[2 * i])

    @pl.loop(0, terms)
    def _(i):
        send(work[PAIR, i], work[PAIR, i]).wait()

    @pl.loop(0, blanks)
    def _(i):
        send(work[BLANK, i], pairs).wait()


def clear_kernel(after, out, done, blank, sems):
    done[...] = jnp.full(done.shape, after[0, 0], jnp.int32)
    count = blank.shape[0]
    blank[...] = jnp.zeros(blank.shape, jnp.float32)
    copies = [
        pltpu.make_async_copy(blank, out.at[c * count : (c + 1) * count], sems.at[c])
        for c in range(CLEARS)
    ]
    for c in copies:
        c.start()
    for c in copies:
        c.wait()


def dot3(a, b):
    def dot(left, right):
        return jnp.dot(left, right, preferred_element_type=jnp.float32)

    return dot(a[0], b[0]) + (dot(a[0], b[1]) + dot(a[1], b[0]))


def tile(full, row, col):
    return full[row * 8 : row * 8 + 8, col * LANES : (col + 1) * LANES]


def blocks(rows):
    return jnp.concatenate([jnp.concatenate(r, axis=1) for r in rows], axis=0)


def potential_of(density, x, xt, z, zt, y, yt, weights):
    pairs_x = MODES // 16
    u = dot3(x, split(density))
    u = blocks(
        [[tile(u, 2 * tp + par, q) for par in range(2)] for tp in range(pairs_x) for q in range(8)]
    )
    u = dot3(split(u), z)
    u = blocks(
        [[tile(u, tp * 8 + q, g) for tp in range(pairs_x)] for g in range(4) for q in range(8)]
    )
    u = dot3(y, split(u)) * weights
    u = dot3(yt, split(u))
    u = blocks(
        [[tile(u, g * 8 + q, tp) for g in range(4)] for tp in range(pairs_x) for q in range(8)]
    )
    u = dot3(split(u), zt)
    u = blocks(
        [[tile(u, tp * 8 + q, par) for q in range(8)] for tp in range(pairs_x) for par in range(2)]
    )
    return dot3(xt, split(u))


def solve_kernel(orb_dev, own, received, cleared, *refs):
    del cleared
    mats, weights, out = refs[:12], *refs[12:]
    n_slab, _, pair_dev, rows, _ = received.shape
    half = n_slab // 2
    for i in range(pair_dev):
        plane = [own[i, side] // orb_dev for side in range(2)]
        sides = [
            jnp.concatenate(
                [received[s, at, i] + received[s + half, at, i] for s in range(half)], axis=0
            )
            for at in plane
        ]
        together = plane[0] == plane[1]
        density = jnp.where(together, sides[0], sides[0] * sides[1])
        m = [(mats[k][i], mats[k + 1][i]) for k in range(0, 12, 2)]
        potential = potential_of(density, *m, weights[...])
        for side in range(2):
            term = jnp.where(together, potential, potential * sides[1 - side])
            for s in range(half):
                part = term[s * rows : (s + 1) * rows]
                out[s, plane[side], i] = part
                out[s + half, plane[side], i] = part


def place_kernel(work, orbitals, returned, zeros, out, held, acc, sems, out_sems):
    del zeros
    place_terms(work, orbitals, lambda at: returned[at], out, held, acc, sems, out_sems)


def place_terms(work, orbitals, fetch, out, held, acc, sems, out_sems):
    _, slab_rows, _ = orbitals.shape
    terms, first_row = work[COUNT, 0], work[COUNT, 1]

    def factors(i):
        return [
            pltpu.make_async_copy(
                orbitals.at[work[which, i]], held.at[2 * i + n], sems.at[2 * i + n]
            )
            for n, which in enumerate((SLOT, SECOND))
        ]

    def copy_out(k):
        return pltpu.make_async_copy(acc.at[k], out.at[k], out_sems.at[k])

    @pl.loop(0, terms)
    def _(i):
        @pl.when(work[SECOND, i] >= 0)
        def _():
            for c in factors(i):
                c.start()

    @pl.loop(0, terms)
    def _(i):
        a, b = work[SLOT, i], work[SECOND, i]
        mask = row_mask(first_row, slab_rows, work[START_X, i])
        pieces = unfold(fetch(work[PAIR, i]), work[START_Y, i], work[START_Z, i], mask)

        def add(k, later, last, slot):
            def term(v):
                if slot is None:
                    return pieces[v]
                return pieces[v] * held[slot, :, v * LANES : (v + 1) * LANES]

            @pl.when(later == 0)
            def _():
                for v in range(len(pieces)):
                    acc[k, :, v * LANES : (v + 1) * LANES] = term(v)

            @pl.when(later != 0)
            def _():
                for v in range(len(pieces)):
                    acc[k, :, v * LANES : (v + 1) * LANES] += term(v)

            @pl.when(last != 0)
            def _():
                copy_out(k).start()

        @pl.when(b >= 0)
        def _():
            for c in factors(i):
                c.wait()
            add(a, work[FIRST_A, i], work[LAST_A, i], 2 * i + 1)
            add(b, work[FIRST_B, i], work[LAST_B, i], 2 * i)

        @pl.when(b < 0)
        def _():
            add(a, work[FIRST_A, i], work[LAST_A, i], None)

    @pl.loop(0, terms)
    def _(i):
        @pl.when(work[LAST_A, i] != 0)
        def _():
            copy_out(work[SLOT, i]).wait()

        @pl.when((work[SECOND, i] >= 0) & (work[LAST_B, i] != 0))
        def _():
            copy_out(work[SECOND, i]).wait()


def quotient(value, by):
    return value >> (by.bit_length() - 1) if by & (by - 1) == 0 else value // by


def pick(begins, parts, index, act):
    for begin, part in zip(begins, parts, strict=True):
        inside = (index >= begin) & (index < begin + part.shape[0])
        pl.when(inside)(lambda part=part, begin=begin: act(part, index - begin))


def slab_fields(n_slab, slab_rows):
    if n_slab > 8:
        return np.ones((FULL,), np.int32), 0
    bits = np.zeros((FULL,), np.int64)
    for x in range(FULL):
        for slab in range(n_slab):
            ends = (slab * slab_rows, (slab + 1) * slab_rows - 1)
            if any((e - x) % FULL < HALF for e in ends):
                bits[x] += 1 << (4 * slab)
    return bits.astype(np.uint32).view(np.int32), 4


def crossing_slots(cap, n_orb):
    near = max(cap * 3 // 4, 1)
    far = max(cap * 3 // 8, 1)
    return [(near, 0) if d == 1 else (far, max(cap // 2 - far, 1)) for d in range(1, n_orb)]


def route_kernel(
    pair_dev, n_orb, width, table_in, fields, orbitals, *refs
):
    *sends, own, work, table, held, seen, load, pieces, crossing, chosen, sems, table_sem = refs
    orb_dev, slab_rows, _ = orbitals.shape
    pairs = table.shape[0] * pair_dev
    cap = own.shape[0]
    spans = crossing_slots(cap, n_orb)
    slots = [sum(span) for span in spans]
    begins = [0] + [cap + sum(slots[:d]) for d in range(n_orb - 1)]
    begins += [begins[d + 1] for d, span in enumerate(spans) if span[1]]
    me = lax.axis_index("orb")
    slab = lax.axis_index("slab")
    base, first_row = me * orb_dev, slab * slab_rows
    table_copy = pltpu.make_async_copy(table_in, table, table_sem)
    table_copy.start()
    for k in range(orb_dev + 1):
        seen[k] = 0
    for k in range(n_orb):
        load[k] = 0
    for k in range(n_orb * n_orb):
        pieces[k] = 0
        crossing[k] = 0
    table_copy.wait()

    def copy_of(index, slot):
        return pltpu.make_async_copy(orbitals.at[index], held.at[slot], sems.at[slot])

    def scan(g, terms):
        row, off = g // pair_dev, (g % pair_dev) * FIELDS
        left, right = table[row, off], table[row, off + 1]
        x, y, z = (table[row, off + 2 + d] for d in range(3))
        a, b = quotient(left, orb_dev), quotient(right, orb_dev)
        weight = jnp.where((a ^ b) == 1, 0, 2)
        load_a, load_b = load[a], load[b]
        cost_a = jnp.where(load_a < cap, load_a + weight * pieces[b * n_orb + a], BIG)
        cost_b = jnp.where(load_b < cap, load_b + weight * pieces[a * n_orb + b], BIG)
        chosen[0] = jnp.where(cost_a <= cost_b, a, b)

        @pl.when((load_a >= cap) & (load_b >= cap))
        def _():
            least = jnp.int32(0)
            for o in range(1, n_orb):
                least = jnp.where(load[o] < load[least], o, least)
            chosen[0] = least

        k = chosen[0]
        j = load[k]
        load[k] = j + 1
        here = fields[x]
        meets = in_box(first_row, x) | in_box(first_row + slab_rows - 1, x)

        def cross(o, used):
            at = o * n_orb + k
            taken = crossing[at]
            crossing[at] = taken + jnp.where(used, here, 0)
            pieces[at] = pieces[at] + jnp.where(used, 1, 0)
            count = (taken >> (width * slab)) & 15 if width else taken
            d = o ^ k
            begin, room = jnp.int32(cap), jnp.int32(slots[0])
            for n in range(1, len(slots)):
                begin = jnp.where(d == n + 1, cap + sum(slots[:n]), begin)
                room = jnp.where(d == n + 1, slots[n], room)
            return begin + jnp.minimum(count, room - 1)

        away_a = a != k
        away_b = (b != k) & (a != b)
        at_a = cross(a, away_a)
        at_b = cross(b, away_b)
        mine = k == me

        @pl.when(mine)
        def _():
            both_away = away_a & away_b
            work[OWN_A, j] = jnp.where(both_away | (away_a & (a == b)), at_a, j)
            work[OWN_B, j] = jnp.where(away_b, at_b, jnp.where(away_a & (a != b), at_a, -1))
            work[OWN_MEETS, j] = jnp.where(meets, 1, 0)
            work[OWN_X, j] = x
            work[OWN_Y, j] = y
            work[OWN_Z, j] = z

        has_left, has_right = a == me, b == me
        live = (has_left | has_right) & meets
        both = has_left & has_right
        first = jnp.where(has_left, left, right) - base
        second = jnp.where(both, right - base, -1)
        work[PAIR, terms] = jnp.where(mine, j, jnp.where(has_left, at_a, at_b))
        work[SLOT, terms] = first
        work[SECOND, terms] = second
        work[START_X, terms] = x
        work[START_Y, terms] = y
        work[START_Z, terms] = z

        @pl.when(live)
        def _():
            copy_of(first, 2 * terms).start()

            @pl.when(both)
            def _():
                copy_of(second, 2 * terms + 1).start()

        for which, index, used in ((FIRST_A, first, live), (FIRST_B, second, live & both)):
            index = jnp.where(used, index, orb_dev)
            work[which, terms] = seen[index]
            seen[index] = 1
        return terms + jnp.where(live, 1, 0)

    terms = lax.fori_loop(0, pairs, scan, jnp.int32(0), unroll=2)
    level = jnp.int32(0)
    for o in range(n_orb):
        for k in range(n_orb):
            if o != k:
                (base_room, more), count = spans[(o ^ k) - 1], crossing[o * n_orb + k]
                for f in range(8 if width else 1):
                    held_here = (count >> (width * f)) & 15 if width else count
                    if more:
                        level = jnp.maximum(level, jnp.where(held_here > base_room, 1, 0))
                    level = jnp.maximum(level, jnp.where(held_here > base_room + more, 2, 0))
    work[COUNT, 0] = terms
    work[COUNT, 1] = first_row
    work[COUNT, 2] = level
    mark_last(work, seen, terms, orb_dev)

    @pl.loop(0, terms)
    def _(i):
        def put(full):
            mask = row_mask(first_row, slab_rows, work[START_X, i])
            folded = [
                jnp.where(mask, piece, 0.0)
                for piece in fold(full, work[START_Y, i], work[START_Z, i])
            ]

            def store(ref, n):
                for q, piece in enumerate(folded):
                    ref[n, :, q * LANES : (q + 1) * LANES] = piece

            pick(begins, [own, *sends], work[PAIR, i], store)

        copy_of(work[SLOT, i], 2 * i).wait()

        @pl.when(work[SECOND, i] >= 0)
        def _():
            copy_of(work[SECOND, i], 2 * i + 1).wait()
            put(held[2 * i] * held[2 * i + 1])

        @pl.when(work[SECOND, i] < 0)
        def _():
            put(held[2 * i])


def density_kernel(begins, work, *refs):
    *parts, out, start_y, side = refs
    pair_dev = start_y.shape[1]
    for i in range(pair_dev):
        start_y[0, i] = work[OWN_Y, lax.axis_index("slab") * pair_dev + i]

    def load(ref, n):
        side[...] = ref[n]

    @pl.loop(0, out.shape[0])
    def _(j):
        a, b = work[OWN_A, j], work[OWN_B, j]
        meets = work[OWN_MEETS, j] != 0

        @pl.when(meets)
        def _():
            pick(begins, parts, a, load)

        def both(ref, n):
            out[j] = side[...] * ref[n]

        @pl.when(meets & (b >= 0))
        def _():
            pick(begins, parts, b, both)

        @pl.when(meets & (b < 0))
        def _():
            out[j] = side[...]

        @pl.when(jnp.logical_not(meets))
        def _():
            out[j] = jnp.zeros(out.shape[1:], jnp.float32)


def plane_solve_kernel(received, *refs):
    mats, weights, out = refs[:12], *refs[12:]
    n_slab, pair_dev, rows, _ = received.shape
    half = n_slab // 2
    for i in range(pair_dev):
        density = jnp.concatenate(
            [received[s, i] + received[s + half, i] for s in range(half)], axis=0
        )
        m = [(mats[k][i], mats[k + 1][i]) for k in range(0, 12, 2)]
        potential = potential_of(density, *m, weights[...])
        for s in range(half):
            part = potential[s * rows : (s + 1) * rows]
            out[s, i] = part
            out[s + half, i] = part


def term_kernel(begins, work, potential, *refs):
    count = (len(refs) - 2) // 2
    parts, outs = refs[:count], refs[count : 2 * count]
    after, term = refs[-2:]
    after[0, 0] = work[COUNT, 0]

    def store(ref, n):
        ref[n] = term[...]

    @pl.loop(0, potential.shape[0])
    def _(j):
        a, b = work[OWN_A, j], work[OWN_B, j]
        meets = work[OWN_MEETS, j] != 0

        def times(ref, n):
            term[...] = potential[j] * ref[n]

        @pl.when(meets & (b >= 0))
        def _():
            for source, target in ((a, b), (b, a)):
                pick(begins, parts, source, times)
                pick(begins, outs, target, store)

        @pl.when(meets & (b < 0))
        def _():
            term[...] = potential[j]
            pick(begins, outs, a, store)


def plane_place_kernel(begins, work, orbitals, zeros, *refs):
    del zeros
    *parts, out, held, acc, term, sems, out_sems = refs

    def load(ref, n):
        term[...] = ref[n]

    def fetch(at):
        pick(begins, parts, at, load)
        return term[...]

    place_terms(work, orbitals, fetch, out, held, acc, sems, out_sems)


def body(orbitals, pair_list, box_start):
    n_slab = lax.axis_size("slab")
    n_orb = lax.axis_size("orb")
    axes = ("slab", "orb")
    orb_dev, slab_rows, cells = orbitals.shape
    pair_dev = pair_list.shape[0]
    devices = n_slab * n_orb
    pairs = devices * pair_dev

    smem = pl.BlockSpec(memory_space=pltpu.SMEM)
    vmem = pl.BlockSpec(memory_space=pltpu.VMEM)
    free = pl.BlockSpec(memory_space=pl.ANY)
    hbm = pl.BlockSpec(memory_space=pltpu.HBM)
    slots = (pairs, slab_rows, PACKED)
    held = pltpu.VMEM((2 * pairs, slab_rows, cells), jnp.float32)

    def grant(mib):
        return pltpu.CompilerParams(vmem_limit_bytes=mib * MIB)

    width = -(-pair_dev * FIELDS // LANES) * LANES
    row = jnp.concatenate([pair_list, box_start], axis=1)
    row = jnp.pad(row, ((0, 0), (0, FIELDS - row.shape[1]))).reshape(1, pair_dev * FIELDS)
    row = jnp.pad(row, ((0, 0), (0, width - row.shape[1])))
    table = lax.all_to_all(
        jnp.broadcast_to(row, (devices, width)), axes, split_axis=0, concat_axis=0, tiled=True
    )

    cap = pairs // n_orb
    spans = crossing_slots(cap, n_orb)
    rooms = [sum(span) for span in spans]
    begins = [0] + [cap + sum(rooms[:d]) for d in range(n_orb - 1)]
    fields, field_bits = slab_fields(n_slab, slab_rows)
    lists = jax.ShapeDtypeStruct((FULL_ROWS, -(-(2 * pairs + 1) // LANES) * LANES), jnp.int32)
    one_plane = jax.ShapeDtypeStruct((cap, slab_rows, PACKED), jnp.float32)

    def crossed(level):
        return [
            jax.ShapeDtypeStruct((sum(span[: level + 1]), slab_rows, PACKED), jnp.float32)
            for span in spans
        ]

    fewer = [d for d, span in enumerate(spans) if span[1]]
    leaving = crossed(1) + [crossed(0)[d] for d in fewer]
    one_slot = pltpu.VMEM((slab_rows, PACKED), jnp.float32)

    def cross(parts):
        return [
            lax.ppermute(part, "orb", [(o, o ^ (n + 1)) for o in range(n_orb)])
            for n, part in enumerate(parts)
        ]

    def clear(work):
        return pl.pallas_call(
            clear_kernel,
            out_shape=[
                jax.ShapeDtypeStruct(orbitals.shape, jnp.float32),
                jax.ShapeDtypeStruct((8, LANES), jnp.int32),
            ],
            in_specs=[smem],
            out_specs=[hbm, vmem],
            scratch_shapes=[
                pltpu.VMEM((orb_dev // CLEARS, slab_rows, cells), jnp.float32),
                pltpu.SemaphoreType.DMA((CLEARS,)),
            ],
            compiler_params=grant(16),
            cost_estimate=pl.CostEstimate(
                flops=0, bytes_accessed=orbitals.size * 4, transcendentals=0
            ),
            name="clear",
        )(work)

    *sends, own_pieces, work = pl.pallas_call(
        functools.partial(route_kernel, pair_dev, n_orb, field_bits),
        out_shape=[*leaving, one_plane, lists],
        in_specs=[free, smem, hbm],
        out_specs=[vmem] * (len(leaving) + 1) + [smem],
        scratch_shapes=[
            pltpu.SMEM((devices, width), jnp.int32),
            held,
            pltpu.SMEM((orb_dev + 1,), jnp.int32),
            pltpu.SMEM((n_orb,), jnp.int32),
            pltpu.SMEM((n_orb * n_orb,), jnp.int32),
            pltpu.SMEM((n_orb * n_orb,), jnp.int32),
            pltpu.SMEM((1,), jnp.int32),
            pltpu.SemaphoreType.DMA((2 * pairs,)),
            pltpu.SemaphoreType.DMA,
        ],
        compiler_params=grant(56),
        name="route",
    )(table, jnp.asarray(fields), orbitals)

    def in_planes(level, table, orbitals, box_start, work, own_pieces, *sends):
        del table, box_start
        sends, short = list(sends[: n_orb - 1]), sends[n_orb - 1 :]
        if level == 0:
            for d, part in zip(fewer, short):
                sends[d] = part
        arrived = cross(sends)
        starts = lax.dynamic_slice(
            work, (OWN_X, lax.axis_index("slab") * pair_dev), (3, pair_dev)
        )
        density, start_y = pl.pallas_call(
            functools.partial(density_kernel, begins),
            out_shape=[one_plane, jax.ShapeDtypeStruct((1, pair_dev), jnp.int32)],
            in_specs=[smem] + [vmem] * n_orb,
            out_specs=[vmem, smem],
            scratch_shapes=[one_slot],
            compiler_params=grant(8),
            name="density",
        )(work, own_pieces, *arrived)
        mats = matrices(starts[0], start_y[0], starts[2])
        received = lax.all_to_all(density, "slab", split_axis=0, concat_axis=0, tiled=True)
        by_slab = (n_slab, pair_dev, slab_rows, PACKED)
        solved = pl.pallas_call(
            plane_solve_kernel,
            out_shape=jax.ShapeDtypeStruct(by_slab, jnp.float32),
            in_specs=[vmem] * 14,
            out_specs=vmem,
            compiler_params=grant(16),
            name="solve",
        )(received.reshape(by_slab), *mats, jnp.asarray(spectrum()))
        potential = lax.all_to_all(
            solved.reshape(one_plane.shape), "slab", split_axis=0, concat_axis=0, tiled=True
        )
        own_terms, *sends, after = pl.pallas_call(
            functools.partial(term_kernel, begins),
            out_shape=[one_plane, *crossed(level), jax.ShapeDtypeStruct((1, 1), jnp.int32)],
            in_specs=[smem, vmem] + [vmem] * n_orb,
            out_specs=[vmem] * n_orb + [smem],
            scratch_shapes=[one_slot],
            compiler_params=grant(8),
            name="terms",
        )(work, potential, own_pieces, *arrived)
        arrived = cross(sends)
        zeros, _ = clear(after)
        return pl.pallas_call(
            functools.partial(plane_place_kernel, begins),
            out_shape=jax.ShapeDtypeStruct(orbitals.shape, jnp.float32),
            in_specs=[smem, hbm, hbm] + [vmem] * n_orb,
            out_specs=hbm,
            scratch_shapes=[
                held,
                pltpu.VMEM(orbitals.shape, jnp.float32),
                one_slot,
                pltpu.SemaphoreType.DMA((2 * pairs,)),
                pltpu.SemaphoreType.DMA((orb_dev,)),
            ],
            input_output_aliases={2: 0},
            compiler_params=grant(52),
            name="place",
        )(work, orbitals, zeros, own_terms, *arrived)

    def direct(table, orbitals, box_start, *unused):
        del unused
        outgoing, work = pl.pallas_call(
            functools.partial(pack_kernel, pair_dev),
            out_shape=[
                jax.ShapeDtypeStruct(slots, jnp.float32),
                lists,
            ],
            in_specs=[free, hbm],
            out_specs=[hbm, smem],
            scratch_shapes=[
                pltpu.SMEM((devices, width), jnp.int32),
                held,
                pltpu.VMEM((pairs + 1, slab_rows, PACKED), jnp.float32),
                pltpu.SMEM((orb_dev + 1,), jnp.int32),
                pltpu.SemaphoreType.DMA((2 * pairs,)),
                pltpu.SemaphoreType.DMA((pairs,)),
                pltpu.SemaphoreType.DMA,
            ],
            compiler_params=grant(56),
            name="pack",
        )(table, orbitals)
        received = lax.all_to_all(outgoing, axes, split_axis=0, concat_axis=0, tiled=True)

        zeros, cleared = clear(work)

        solved = pl.pallas_call(
            functools.partial(solve_kernel, orb_dev),
            out_shape=jax.ShapeDtypeStruct((n_slab, n_orb, pair_dev, slab_rows, PACKED), jnp.float32),
            in_specs=[smem] + [vmem] * 15,
            out_specs=vmem,
            compiler_params=grant(16),
            name="solve",
        )(
            pair_list,
            received.reshape(n_slab, n_orb, pair_dev, slab_rows, PACKED),
            cleared,
            *matrices(*box_start.T),
            jnp.asarray(spectrum()),
        )
        returned = lax.all_to_all(solved.reshape(slots), axes, split_axis=0, concat_axis=0, tiled=True)

        return pl.pallas_call(
            place_kernel,
            out_shape=jax.ShapeDtypeStruct(orbitals.shape, jnp.float32),
            in_specs=[smem, hbm, vmem, hbm],
            out_specs=hbm,
            scratch_shapes=[
                held,
                pltpu.VMEM(orbitals.shape, jnp.float32),
                pltpu.SemaphoreType.DMA((2 * pairs,)),
                pltpu.SemaphoreType.DMA((orb_dev,)),
            ],
            input_output_aliases={3: 0},
            compiler_params=grant(52),
            name="place",
        )(work, orbitals, returned, zeros)

    return lax.switch(
        work[COUNT, 2],
        [functools.partial(in_planes, 0), functools.partial(in_planes, 1), direct],
        table,
        orbitals,
        box_start,
        work,
        own_pieces,
        *sends,
    )


def solution(mesh):
    return jax.shard_map(
        body,
        mesh=mesh,
        in_specs=(P("orb", "slab", None), P(("slab", "orb"), None), P(("slab", "orb"), None)),
        out_specs=P("orb", "slab", None),
        check_vma=False,
    )
```

```python
import functools

import jax
import jax.numpy as jnp
import numpy as np
from jax import lax
from jax.experimental import pallas as pl
from jax.experimental.pallas import tpu as pltpu
from jax.sharding import PartitionSpec as P

NY = 64
NZ = 64
ITERS = 16
HALF = 32
FULL = 64
PACKED = HALF * HALF
MODES = 48
MARGIN = (MODES - HALF) // 2
PERIOD = 2 * (MODES + 1)
LANES = 128
FIELDS = 8
CLEARS = 16
MIB = 1024 * 1024
COUNT, PAIR, SLOT, SECOND, FIRST_A, FIRST_B, LAST_A, LAST_B, START_X, START_Y, START_Z, BLANK = range(12)
OWN_A, OWN_B, OWN_MEETS, OWN_X, OWN_Y, OWN_Z = range(12, 18)
FULL_ROWS = 24
BIG = 1 << 20

screening = 0.02
center_eig = 6.0 + screening
half_width = 6.0
sigma_one = center_eig / half_width


def spectrum():
    cosine = np.cos(np.pi * (np.arange(MODES) + 1) / (MODES + 1))
    lam = center_eig - 2.0 * (
        cosine[:, None, None] + cosine[None, :, None] + cosine[None, None, :]
    )
    solution_now, residue, ratio = np.zeros_like(lam), np.ones_like(lam), 1.0 / sigma_one
    update = residue / center_eig
    for _ in range(ITERS):
        solution_now = solution_now + update
        residue = residue - lam * update
        ratio_next = 1.0 / (2.0 * sigma_one - ratio)
        update = ratio_next * ratio * update + 2.0 * ratio_next / half_width * residue
        ratio = ratio_next
    table = -solution_now * (2.0 / (MODES + 1)) ** 3
    table = np.pad(table, ((0, 0), (0, 0), (0, LANES // 2 - MODES)))
    table = table.reshape(MODES // 16, 2, 8, MODES, LANES // 2).transpose(3, 2, 0, 1, 4)
    return table.reshape(MODES * 8, MODES // 16 * LANES).astype(np.float32)


def sine(mode, cell, start):
    place = (cell - start) & (HALF - 1)
    phase = ((mode + 1) * (place + MARGIN + 1)) % PERIOD
    return jnp.sin(phase.astype(jnp.float32) * np.float32(np.pi / (MODES + 1)))


def split(full):
    high = full.astype(jnp.bfloat16)
    return high, (full - high.astype(jnp.float32)).astype(jnp.bfloat16)


def halves(full):
    high = lax.reduce_precision(full, 8, 7)
    return high.astype(jnp.bfloat16), (full - high).astype(jnp.bfloat16)


def iotas(shape):
    return [lax.broadcasted_iota(jnp.int32, shape, d) for d in range(len(shape))]


def cell_y(q, g):
    return 2 * q + (g >> 1) + HALF // 2 * (g & 1)


def matrices(*starts):
    count = starts[0].shape[0]
    bx, by, bz = (start[:, None, None] for start in starts)

    def x_of(k, r):
        return sine(k, r, bx)

    def y_of(row, col):
        g, q = col >> 6, (col >> 3) & 7
        return jnp.where((row & 7) == (col & 7), sine(row >> 3, cell_y(q, g), by), 0.0)

    def z_of(row, col):
        same = ((row >> 7) == ((col >> 6) & 1)) & (((row >> 5) & 3) == (col >> 7))
        kz = col & 63
        return jnp.where(same & (kz < MODES), sine(kz, row & 31, bz), 0.0)

    out = []
    for of, rows, cols in ((x_of, MODES, HALF), (z_of, 256, 512), (y_of, MODES * 8, 256)):
        _, row, col = iotas((count, rows, cols))
        out += halves(of(row, col))
        _, row, col = iotas((count, cols, rows))
        out += halves(of(col, row))
    return out


def lane(shape):
    return lax.broadcasted_iota(jnp.int32, shape, len(shape) - 1)


def in_box(cell, start):
    return ((cell - start) & (FULL - 1)) < HALF


def fold(full, start_y, start_z):
    rows = full.shape[0]
    at = lane((rows, LANES))
    upper = (at >> 6) & 1
    in_z = in_box(at & 31, start_z)
    first = (at & 63) < 32
    picked = []
    for v in range(HALF // 2):
        low = full[:, v * LANES : (v + 1) * LANES]
        high = full[:, (v + HALF // 2) * LANES : (v + HALF // 2 + 1) * LANES]
        picked.append(jnp.where(in_box(2 * v + upper, start_y), low, high))
    out = []
    for q in range(8):
        a, b = picked[q], picked[q + 8]
        a = jnp.where(in_z, a, pltpu.roll(a, 96, 1))
        b = jnp.where(in_z, pltpu.roll(b, 32, 1), b)
        out.append(jnp.where(first, a, b))
    return out


def unfold(packed, start_y, start_z, row_mask):
    rows = packed.shape[0]
    at = lane((rows, LANES))
    upper = (at >> 6) & 1
    inside = in_box(at & 63, start_z) & row_mask
    first = (at & 63) < 32
    out = [None] * 32
    for v in range(16):
        piece = packed[:, (v % 8) * LANES : (v % 8 + 1) * LANES]
        if v < 8:
            wide = jnp.where(first, piece, pltpu.roll(piece, 32, 1))
        else:
            wide = jnp.where(first, pltpu.roll(piece, 96, 1), piece)
        wide = jnp.where(inside, wide, 0.0)
        in_y = in_box(2 * v + upper, start_y)
        out[v] = jnp.where(in_y, wide, 0.0)
        out[v + 16] = jnp.where(in_y, 0.0, wide)
    return out


def row_mask(first_row, rows, start_x):
    at = lax.broadcasted_iota(jnp.int32, (rows, LANES), 0)
    return in_box(at + first_row, start_x)


def mark_last(work, seen, terms, orb_dev):
    @pl.loop(0, terms)
    def _(n):
        i = terms - 1 - n
        for which, source in ((LAST_B, SECOND), (LAST_A, SLOT)):
            k = work[source, i]
            k = jnp.where(k < 0, orb_dev, k)
            work[which, i] = seen[k]
            seen[k] = 0


def pack_kernel(pair_dev, table_in, orbitals, out, work, table, held, packed, seen, sems, out_sems, table_sem):
    orb_dev, slab_rows, _ = orbitals.shape
    pairs = out.shape[0]
    base, first_row = lax.axis_index("orb") * orb_dev, lax.axis_index("slab") * slab_rows
    table_copy = pltpu.make_async_copy(table_in, table, table_sem)
    table_copy.start()
    packed[pairs] = jnp.zeros(packed.shape[1:], jnp.float32)
    for k in range(orb_dev + 1):
        seen[k] = 0
    table_copy.wait()

    def copy_of(index, slot):
        return pltpu.make_async_copy(orbitals.at[index], held.at[slot], sems.at[slot])

    def send(g, source):
        return pltpu.make_async_copy(packed.at[source], out.at[g], out_sems.at[g])

    def scan(g, carry):
        terms, blanks = carry
        row, off = g // pair_dev, (g % pair_dev) * FIELDS
        left, right = table[row, off] - base, table[row, off + 1] - base
        x = table[row, off + 2]
        meets = in_box(first_row, x) | in_box(first_row + slab_rows - 1, x)
        has_left = (left >= 0) & (left < orb_dev)
        has_right = (right >= 0) & (right < orb_dev)
        here = has_left | has_right
        live = here & meets
        both = has_left & has_right
        a = jnp.where(has_left, left, right)
        b = jnp.where(both, right, -1)
        work[PAIR, terms] = g
        work[SLOT, terms] = a
        work[SECOND, terms] = b
        work[START_X, terms] = x
        work[START_Y, terms] = table[row, off + 3]
        work[START_Z, terms] = table[row, off + 4]
        work[BLANK, blanks] = g

        @pl.when(live)
        def _():
            copy_of(a, 2 * terms).start()

            @pl.when(both)
            def _():
                copy_of(b, 2 * terms + 1).start()

        for which, k, used in ((FIRST_A, a, live), (FIRST_B, b, live & both)):
            k = jnp.where(used, k, orb_dev)
            old = seen[k]
            work[which, terms] = old
            seen[k] = 1
        terms = terms + jnp.where(live, 1, 0)
        return terms, blanks + jnp.where(here & jnp.logical_not(meets), 1, 0)

    zero = jnp.int32(0)
    terms, blanks = lax.fori_loop(0, pairs, scan, (zero, zero), unroll=4)
    work[COUNT, 0] = terms
    work[COUNT, 1] = first_row

    @pl.loop(0, blanks)
    def _(i):
        send(work[BLANK, i], pairs).start()

    mark_last(work, seen, terms, orb_dev)

    @pl.loop(0, terms)
    def _(i):
        g = work[PAIR, i]

        def put(full):
            mask = row_mask(first_row, slab_rows, work[START_X, i])
            for q, piece in enumerate(fold(full, work[START_Y, i], work[START_Z, i])):
                packed[g, :, q * LANES : (q + 1) * LANES] = jnp.where(mask, piece, 0.0)
            send(g, g).start()

        copy_of(work[SLOT, i], 2 * i).wait()

        @pl.when(work[SECOND, i] >= 0)
        def _():
            copy_of(work[SECOND, i], 2 * i + 1).wait()
            put(held[2 * i] * held[2 * i + 1])

        @pl.when(work[SECOND, i] < 0)
        def _():
            put(held[2 * i])

    @pl.loop(0, terms)
    def _(i):
        send(work[PAIR, i], work[PAIR, i]).wait()

    @pl.loop(0, blanks)
    def _(i):
        send(work[BLANK, i], pairs).wait()


def clear_kernel(after, out, done, blank, sems):
    done[...] = jnp.full(done.shape, after[0, 0], jnp.int32)
    count = blank.shape[0]
    blank[...] = jnp.zeros(blank.shape, jnp.float32)
    copies = [
        pltpu.make_async_copy(blank, out.at[c * count : (c + 1) * count], sems.at[c])
        for c in range(CLEARS)
    ]
    for c in copies:
        c.start()
    for c in copies:
        c.wait()


def dot3(a, b):
    def dot(left, right):
        return jnp.dot(left, right, preferred_element_type=jnp.float32)

    return dot(a[0], b[0]) + (dot(a[0], b[1]) + dot(a[1], b[0]))


def tile(full, row, col):
    return full[row * 8 : row * 8 + 8, col * LANES : (col + 1) * LANES]


def blocks(rows):
    return jnp.concatenate([jnp.concatenate(r, axis=1) for r in rows], axis=0)


def potential_of(density, x, xt, z, zt, y, yt, weights):
    pairs_x = MODES // 16
    u = dot3(x, split(density))
    u = blocks(
        [[tile(u, 2 * tp + par, q) for par in range(2)] for tp in range(pairs_x) for q in range(8)]
    )
    u = dot3(split(u), z)
    u = blocks(
        [[tile(u, tp * 8 + q, g) for tp in range(pairs_x)] for g in range(4) for q in range(8)]
    )
    u = dot3(y, split(u)) * weights
    u = dot3(yt, split(u))
    u = blocks(
        [[tile(u, g * 8 + q, tp) for g in range(4)] for tp in range(pairs_x) for q in range(8)]
    )
    u = dot3(split(u), zt)
    u = blocks(
        [[tile(u, tp * 8 + q, par) for q in range(8)] for tp in range(pairs_x) for par in range(2)]
    )
    return dot3(xt, split(u))


def solve_kernel(orb_dev, own, received, cleared, *refs):
    del cleared
    mats, weights, out = refs[:12], *refs[12:]
    n_slab, _, pair_dev, rows, _ = received.shape
    half = n_slab // 2
    for i in range(pair_dev):
        plane = [own[i, side] // orb_dev for side in range(2)]
        sides = [
            jnp.concatenate(
                [received[s, at, i] + received[s + half, at, i] for s in range(half)], axis=0
            )
            for at in plane
        ]
        together = plane[0] == plane[1]
        density = jnp.where(together, sides[0], sides[0] * sides[1])
        m = [(mats[k][i], mats[k + 1][i]) for k in range(0, 12, 2)]
        potential = potential_of(density, *m, weights[...])
        for side in range(2):
            term = jnp.where(together, potential, potential * sides[1 - side])
            for s in range(half):
                part = term[s * rows : (s + 1) * rows]
                out[s, plane[side], i] = part
                out[s + half, plane[side], i] = part


def place_kernel(work, orbitals, returned, zeros, out, held, acc, sems, out_sems):
    del zeros
    place_terms(work, orbitals, lambda at: returned[at], out, held, acc, sems, out_sems)


def place_terms(work, orbitals, fetch, out, held, acc, sems, out_sems):
    _, slab_rows, _ = orbitals.shape
    terms, first_row = work[COUNT, 0], work[COUNT, 1]

    def factors(i):
        return [
            pltpu.make_async_copy(
                orbitals.at[work[which, i]], held.at[2 * i + n], sems.at[2 * i + n]
            )
            for n, which in enumerate((SLOT, SECOND))
        ]

    def copy_out(k):
        return pltpu.make_async_copy(acc.at[k], out.at[k], out_sems.at[k])

    @pl.loop(0, terms)
    def _(i):
        @pl.when(work[SECOND, i] >= 0)
        def _():
            for c in factors(i):
                c.start()

    @pl.loop(0, terms)
    def _(i):
        a, b = work[SLOT, i], work[SECOND, i]
        mask = row_mask(first_row, slab_rows, work[START_X, i])
        pieces = unfold(fetch(work[PAIR, i]), work[START_Y, i], work[START_Z, i], mask)

        def add(k, later, last, slot):
            def term(v):
                if slot is None:
                    return pieces[v]
                return pieces[v] * held[slot, :, v * LANES : (v + 1) * LANES]

            @pl.when(later == 0)
            def _():
                for v in range(len(pieces)):
                    acc[k, :, v * LANES : (v + 1) * LANES] = term(v)

            @pl.when(later != 0)
            def _():
                for v in range(len(pieces)):
                    acc[k, :, v * LANES : (v + 1) * LANES] += term(v)

            @pl.when(last != 0)
            def _():
                copy_out(k).start()

        @pl.when(b >= 0)
        def _():
            for c in factors(i):
                c.wait()
            add(a, work[FIRST_A, i], work[LAST_A, i], 2 * i + 1)
            add(b, work[FIRST_B, i], work[LAST_B, i], 2 * i)

        @pl.when(b < 0)
        def _():
            add(a, work[FIRST_A, i], work[LAST_A, i], None)

    @pl.loop(0, terms)
    def _(i):
        @pl.when(work[LAST_A, i] != 0)
        def _():
            copy_out(work[SLOT, i]).wait()

        @pl.when((work[SECOND, i] >= 0) & (work[LAST_B, i] != 0))
        def _():
            copy_out(work[SECOND, i]).wait()


def quotient(value, by):
    return value >> (by.bit_length() - 1) if by & (by - 1) == 0 else value // by


def pick(begins, parts, index, act):
    for begin, part in zip(begins, parts, strict=True):
        inside = (index >= begin) & (index < begin + part.shape[0])
        pl.when(inside)(lambda part=part, begin=begin: act(part, index - begin))


def slab_fields(n_slab, slab_rows):
    if n_slab > 8:
        return np.ones((FULL,), np.int32), 0
    bits = np.zeros((FULL,), np.int64)
    for x in range(FULL):
        for slab in range(n_slab):
            ends = (slab * slab_rows, (slab + 1) * slab_rows - 1)
            if any((e - x) % FULL < HALF for e in ends):
                bits[x] += 1 << (4 * slab)
    return bits.astype(np.uint32).view(np.int32), 4


def crossing_slots(cap, n_orb):
    near = max(cap * 3 // 4, 1)
    far = max(cap * 3 // 8, 1)
    step = max(cap // 8, 1)
    return [(near, 0, 0) if d == 1 else (far, step, step) for d in range(1, n_orb)]


def route_kernel(
    pair_dev, n_orb, width, table_in, fields, orbitals, *refs
):
    *sends, own, work, table, held, seen, load, pieces, crossing, chosen, sems, table_sem = refs
    orb_dev, slab_rows, _ = orbitals.shape
    pairs = table.shape[0] * pair_dev
    cap = own.shape[0]
    spans = crossing_slots(cap, n_orb)
    slots = [sum(span) for span in spans]
    begins = [0] + [cap + sum(slots[:d]) for d in range(n_orb - 1)]
    fewer = [d for d, span in enumerate(spans) if span[1]]
    begins += [begins[d + 1] for d in fewer] * (len(spans[0]) - 1)
    me = lax.axis_index("orb")
    slab = lax.axis_index("slab")
    base, first_row = me * orb_dev, slab * slab_rows
    table_copy = pltpu.make_async_copy(table_in, table, table_sem)
    table_copy.start()
    for k in range(orb_dev + 1):
        seen[k] = 0
    for k in range(n_orb):
        load[k] = 0
    for k in range(n_orb * n_orb):
        pieces[k] = 0
        crossing[k] = 0
    table_copy.wait()

    def copy_of(index, slot):
        return pltpu.make_async_copy(orbitals.at[index], held.at[slot], sems.at[slot])

    def scan(g, terms):
        row, off = g // pair_dev, (g % pair_dev) * FIELDS
        left, right = table[row, off], table[row, off + 1]
        x, y, z = (table[row, off + 2 + d] for d in range(3))
        a, b = quotient(left, orb_dev), quotient(right, orb_dev)
        weight = jnp.where((a ^ b) == 1, 0, 2)
        load_a, load_b = load[a], load[b]
        cost_a = jnp.where(load_a < cap, load_a + weight * pieces[b * n_orb + a], BIG)
        cost_b = jnp.where(load_b < cap, load_b + weight * pieces[a * n_orb + b], BIG)
        chosen[0] = jnp.where(cost_a <= cost_b, a, b)

        @pl.when((load_a >= cap) & (load_b >= cap))
        def _():
            least = jnp.int32(0)
            for o in range(1, n_orb):
                least = jnp.where(load[o] < load[least], o, least)
            chosen[0] = least

        k = chosen[0]
        j = load[k]
        load[k] = j + 1
        here = fields[x]
        meets = in_box(first_row, x) | in_box(first_row + slab_rows - 1, x)

        def cross(o, used):
            at = o * n_orb + k
            taken = crossing[at]
            crossing[at] = taken + jnp.where(used, here, 0)
            pieces[at] = pieces[at] + jnp.where(used, 1, 0)
            count = (taken >> (width * slab)) & 15 if width else taken
            d = o ^ k
            begin, room = jnp.int32(cap), jnp.int32(slots[0])
            for n in range(1, len(slots)):
                begin = jnp.where(d == n + 1, cap + sum(slots[:n]), begin)
                room = jnp.where(d == n + 1, slots[n], room)
            return begin + jnp.minimum(count, room - 1)

        away_a = a != k
        away_b = (b != k) & (a != b)
        at_a = cross(a, away_a)
        at_b = cross(b, away_b)
        mine = k == me

        @pl.when(mine)
        def _():
            both_away = away_a & away_b
            work[OWN_A, j] = jnp.where(both_away | (away_a & (a == b)), at_a, j)
            work[OWN_B, j] = jnp.where(away_b, at_b, jnp.where(away_a & (a != b), at_a, -1))
            work[OWN_MEETS, j] = jnp.where(meets, 1, 0)
            work[OWN_X, j] = x
            work[OWN_Y, j] = y
            work[OWN_Z, j] = z

        has_left, has_right = a == me, b == me
        live = (has_left | has_right) & meets
        both = has_left & has_right
        first = jnp.where(has_left, left, right) - base
        second = jnp.where(both, right - base, -1)
        work[PAIR, terms] = jnp.where(mine, j, jnp.where(has_left, at_a, at_b))
        work[SLOT, terms] = first
        work[SECOND, terms] = second
        work[START_X, terms] = x
        work[START_Y, terms] = y
        work[START_Z, terms] = z

        @pl.when(live)
        def _():
            copy_of(first, 2 * terms).start()

            @pl.when(both)
            def _():
                copy_of(second, 2 * terms + 1).start()

        for which, index, used in ((FIRST_A, first, live), (FIRST_B, second, live & both)):
            index = jnp.where(used, index, orb_dev)
            work[which, terms] = seen[index]
            seen[index] = 1
        return terms + jnp.where(live, 1, 0)

    terms = lax.fori_loop(0, pairs, scan, jnp.int32(0), unroll=2)
    level = jnp.int32(0)
    for o in range(n_orb):
        for k in range(n_orb):
            if o != k:
                span, count = spans[(o ^ k) - 1], crossing[o * n_orb + k]
                for f in range(8 if width else 1):
                    held_here = (count >> (width * f)) & 15 if width else count
                    for at in range(len(span)):
                        room = sum(span[: at + 1])
                        level = jnp.maximum(level, jnp.where(held_here > room, at + 1, 0))
    work[COUNT, 0] = terms
    work[COUNT, 1] = first_row
    work[COUNT, 2] = level
    mark_last(work, seen, terms, orb_dev)

    @pl.loop(0, terms)
    def _(i):
        def put(full):
            mask = row_mask(first_row, slab_rows, work[START_X, i])
            folded = [
                jnp.where(mask, piece, 0.0)
                for piece in fold(full, work[START_Y, i], work[START_Z, i])
            ]

            def store(ref, n):
                for q, piece in enumerate(folded):
                    ref[n, :, q * LANES : (q + 1) * LANES] = piece

            pick(begins, [own, *sends], work[PAIR, i], store)

        copy_of(work[SLOT, i], 2 * i).wait()

        @pl.when(work[SECOND, i] >= 0)
        def _():
            copy_of(work[SECOND, i], 2 * i + 1).wait()
            put(held[2 * i] * held[2 * i + 1])

        @pl.when(work[SECOND, i] < 0)
        def _():
            put(held[2 * i])


def density_kernel(begins, work, *refs):
    *parts, out, start_y, side = refs
    pair_dev = start_y.shape[1]
    for i in range(pair_dev):
        start_y[0, i] = work[OWN_Y, lax.axis_index("slab") * pair_dev + i]

    def load(ref, n):
        side[...] = ref[n]

    @pl.loop(0, out.shape[0])
    def _(j):
        a, b = work[OWN_A, j], work[OWN_B, j]
        meets = work[OWN_MEETS, j] != 0

        @pl.when(meets)
        def _():
            pick(begins, parts, a, load)

        def both(ref, n):
            out[j] = side[...] * ref[n]

        @pl.when(meets & (b >= 0))
        def _():
            pick(begins, parts, b, both)

        @pl.when(meets & (b < 0))
        def _():
            out[j] = side[...]

        @pl.when(jnp.logical_not(meets))
        def _():
            out[j] = jnp.zeros(out.shape[1:], jnp.float32)


def plane_solve_kernel(received, *refs):
    mats, weights, out = refs[:12], *refs[12:]
    n_slab, pair_dev, rows, _ = received.shape
    half = n_slab // 2
    for i in range(pair_dev):
        density = jnp.concatenate(
            [received[s, i] + received[s + half, i] for s in range(half)], axis=0
        )
        m = [(mats[k][i], mats[k + 1][i]) for k in range(0, 12, 2)]
        potential = potential_of(density, *m, weights[...])
        for s in range(half):
            part = potential[s * rows : (s + 1) * rows]
            out[s, i] = part
            out[s + half, i] = part


def term_kernel(begins, work, potential, *refs):
    count = (len(refs) - 2) // 2
    parts, outs = refs[:count], refs[count : 2 * count]
    after, term = refs[-2:]
    after[0, 0] = work[COUNT, 0]

    def store(ref, n):
        ref[n] = term[...]

    @pl.loop(0, potential.shape[0])
    def _(j):
        a, b = work[OWN_A, j], work[OWN_B, j]
        meets = work[OWN_MEETS, j] != 0

        def times(ref, n):
            term[...] = potential[j] * ref[n]

        @pl.when(meets & (b >= 0))
        def _():
            for source, target in ((a, b), (b, a)):
                pick(begins, parts, source, times)
                pick(begins, outs, target, store)

        @pl.when(meets & (b < 0))
        def _():
            term[...] = potential[j]
            pick(begins, outs, a, store)


def plane_place_kernel(begins, work, orbitals, zeros, *refs):
    del zeros
    *parts, out, held, acc, term, sems, out_sems = refs

    def load(ref, n):
        term[...] = ref[n]

    def fetch(at):
        pick(begins, parts, at, load)
        return term[...]

    place_terms(work, orbitals, fetch, out, held, acc, sems, out_sems)


def body(orbitals, pair_list, box_start):
    n_slab = lax.axis_size("slab")
    n_orb = lax.axis_size("orb")
    axes = ("slab", "orb")
    orb_dev, slab_rows, cells = orbitals.shape
    pair_dev = pair_list.shape[0]
    devices = n_slab * n_orb
    pairs = devices * pair_dev

    smem = pl.BlockSpec(memory_space=pltpu.SMEM)
    vmem = pl.BlockSpec(memory_space=pltpu.VMEM)
    free = pl.BlockSpec(memory_space=pl.ANY)
    hbm = pl.BlockSpec(memory_space=pltpu.HBM)
    slots = (pairs, slab_rows, PACKED)
    held = pltpu.VMEM((2 * pairs, slab_rows, cells), jnp.float32)

    def grant(mib):
        return pltpu.CompilerParams(vmem_limit_bytes=mib * MIB)

    width = -(-pair_dev * FIELDS // LANES) * LANES
    row = jnp.concatenate([pair_list, box_start], axis=1)
    row = jnp.pad(row, ((0, 0), (0, FIELDS - row.shape[1]))).reshape(1, pair_dev * FIELDS)
    row = jnp.pad(row, ((0, 0), (0, width - row.shape[1])))
    table = lax.all_to_all(
        jnp.broadcast_to(row, (devices, width)), axes, split_axis=0, concat_axis=0, tiled=True
    )

    cap = pairs // n_orb
    spans = crossing_slots(cap, n_orb)
    rooms = [sum(span) for span in spans]
    begins = [0] + [cap + sum(rooms[:d]) for d in range(n_orb - 1)]
    fields, field_bits = slab_fields(n_slab, slab_rows)
    lists = jax.ShapeDtypeStruct((FULL_ROWS, -(-(2 * pairs + 1) // LANES) * LANES), jnp.int32)
    one_plane = jax.ShapeDtypeStruct((cap, slab_rows, PACKED), jnp.float32)

    def crossed(level):
        return [
            jax.ShapeDtypeStruct((sum(span[: level + 1]), slab_rows, PACKED), jnp.float32)
            for span in spans
        ]

    fewer = [d for d, span in enumerate(spans) if span[1]]
    top = len(spans[0]) - 1
    leaving = crossed(top) + [crossed(level)[d] for level in range(top) for d in fewer]
    one_slot = pltpu.VMEM((slab_rows, PACKED), jnp.float32)

    def cross(parts):
        return [
            lax.ppermute(part, "orb", [(o, o ^ (n + 1)) for o in range(n_orb)])
            for n, part in enumerate(parts)
        ]

    def clear(work):
        return pl.pallas_call(
            clear_kernel,
            out_shape=[
                jax.ShapeDtypeStruct(orbitals.shape, jnp.float32),
                jax.ShapeDtypeStruct((8, LANES), jnp.int32),
            ],
            in_specs=[smem],
            out_specs=[hbm, vmem],
            scratch_shapes=[
                pltpu.VMEM((orb_dev // CLEARS, slab_rows, cells), jnp.float32),
                pltpu.SemaphoreType.DMA((CLEARS,)),
            ],
            compiler_params=grant(16),
            cost_estimate=pl.CostEstimate(
                flops=0, bytes_accessed=orbitals.size * 4, transcendentals=0
            ),
            name="clear",
        )(work)

    *sends, own_pieces, work = pl.pallas_call(
        functools.partial(route_kernel, pair_dev, n_orb, field_bits),
        out_shape=[*leaving, one_plane, lists],
        in_specs=[free, smem, hbm],
        out_specs=[vmem] * (len(leaving) + 1) + [smem],
        scratch_shapes=[
            pltpu.SMEM((devices, width), jnp.int32),
            held,
            pltpu.SMEM((orb_dev + 1,), jnp.int32),
            pltpu.SMEM((n_orb,), jnp.int32),
            pltpu.SMEM((n_orb * n_orb,), jnp.int32),
            pltpu.SMEM((n_orb * n_orb,), jnp.int32),
            pltpu.SMEM((1,), jnp.int32),
            pltpu.SemaphoreType.DMA((2 * pairs,)),
            pltpu.SemaphoreType.DMA,
        ],
        compiler_params=grant(56),
        name="route",
    )(table, jnp.asarray(fields), orbitals)

    def in_planes(level, table, orbitals, box_start, work, own_pieces, *sends):
        del table, box_start
        sends, short = list(sends[: n_orb - 1]), sends[n_orb - 1 :]
        if level < top:
            for d, part in zip(fewer, short[level * len(fewer) :]):
                sends[d] = part
        arrived = cross(sends)
        starts = lax.dynamic_slice(
            work, (OWN_X, lax.axis_index("slab") * pair_dev), (3, pair_dev)
        )
        density, start_y = pl.pallas_call(
            functools.partial(density_kernel, begins),
            out_shape=[one_plane, jax.ShapeDtypeStruct((1, pair_dev), jnp.int32)],
            in_specs=[smem] + [vmem] * n_orb,
            out_specs=[vmem, smem],
            scratch_shapes=[one_slot],
            compiler_params=grant(8),
            name="density",
        )(work, own_pieces, *arrived)
        mats = matrices(starts[0], start_y[0], starts[2])
        received = lax.all_to_all(density, "slab", split_axis=0, concat_axis=0, tiled=True)
        by_slab = (n_slab, pair_dev, slab_rows, PACKED)
        solved = pl.pallas_call(
            plane_solve_kernel,
            out_shape=jax.ShapeDtypeStruct(by_slab, jnp.float32),
            in_specs=[vmem] * 14,
            out_specs=vmem,
            compiler_params=grant(16),
            name="solve",
        )(received.reshape(by_slab), *mats, jnp.asarray(spectrum()))
        potential = lax.all_to_all(
            solved.reshape(one_plane.shape), "slab", split_axis=0, concat_axis=0, tiled=True
        )
        own_terms, *sends, after = pl.pallas_call(
            functools.partial(term_kernel, begins),
            out_shape=[one_plane, *crossed(level), jax.ShapeDtypeStruct((1, 1), jnp.int32)],
            in_specs=[smem, vmem] + [vmem] * n_orb,
            out_specs=[vmem] * n_orb + [smem],
            scratch_shapes=[one_slot],
            compiler_params=grant(8),
            name="terms",
        )(work, potential, own_pieces, *arrived)
        arrived = cross(sends)
        zeros, _ = clear(after)
        return pl.pallas_call(
            functools.partial(plane_place_kernel, begins),
            out_shape=jax.ShapeDtypeStruct(orbitals.shape, jnp.float32),
            in_specs=[smem, hbm, hbm] + [vmem] * n_orb,
            out_specs=hbm,
            scratch_shapes=[
                held,
                pltpu.VMEM(orbitals.shape, jnp.float32),
                one_slot,
                pltpu.SemaphoreType.DMA((2 * pairs,)),
                pltpu.SemaphoreType.DMA((orb_dev,)),
            ],
            input_output_aliases={2: 0},
            compiler_params=grant(52),
            name="place",
        )(work, orbitals, zeros, own_terms, *arrived)

    def direct(table, orbitals, box_start, *unused):
        del unused
        outgoing, work = pl.pallas_call(
            functools.partial(pack_kernel, pair_dev),
            out_shape=[
                jax.ShapeDtypeStruct(slots, jnp.float32),
                lists,
            ],
            in_specs=[free, hbm],
            out_specs=[hbm, smem],
            scratch_shapes=[
                pltpu.SMEM((devices, width), jnp.int32),
                held,
                pltpu.VMEM((pairs + 1, slab_rows, PACKED), jnp.float32),
                pltpu.SMEM((orb_dev + 1,), jnp.int32),
                pltpu.SemaphoreType.DMA((2 * pairs,)),
                pltpu.SemaphoreType.DMA((pairs,)),
                pltpu.SemaphoreType.DMA,
            ],
            compiler_params=grant(56),
            name="pack",
        )(table, orbitals)
        received = lax.all_to_all(outgoing, axes, split_axis=0, concat_axis=0, tiled=True)

        zeros, cleared = clear(work)

        solved = pl.pallas_call(
            functools.partial(solve_kernel, orb_dev),
            out_shape=jax.ShapeDtypeStruct((n_slab, n_orb, pair_dev, slab_rows, PACKED), jnp.float32),
            in_specs=[smem] + [vmem] * 15,
            out_specs=vmem,
            compiler_params=grant(16),
            name="solve",
        )(
            pair_list,
            received.reshape(n_slab, n_orb, pair_dev, slab_rows, PACKED),
            cleared,
            *matrices(*box_start.T),
            jnp.asarray(spectrum()),
        )
        returned = lax.all_to_all(solved.reshape(slots), axes, split_axis=0, concat_axis=0, tiled=True)

        return pl.pallas_call(
            place_kernel,
            out_shape=jax.ShapeDtypeStruct(orbitals.shape, jnp.float32),
            in_specs=[smem, hbm, vmem, hbm],
            out_specs=hbm,
            scratch_shapes=[
                held,
                pltpu.VMEM(orbitals.shape, jnp.float32),
                pltpu.SemaphoreType.DMA((2 * pairs,)),
                pltpu.SemaphoreType.DMA((orb_dev,)),
            ],
            input_output_aliases={3: 0},
            compiler_params=grant(52),
            name="place",
        )(work, orbitals, returned, zeros)

    return lax.switch(
        work[COUNT, 2],
        [*(functools.partial(in_planes, level) for level in range(top + 1)), direct],
        table,
        orbitals,
        box_start,
        work,
        own_pieces,
        *sends,
    )


def solution(mesh):
    return jax.shard_map(
        body,
        mesh=mesh,
        in_specs=(P("orb", "slab", None), P(("slab", "orb"), None), P(("slab", "orb"), None)),
        out_specs=P("orb", "slab", None),
        check_vma=False,
    )
```

```python
import functools

import jax
import jax.numpy as jnp
import numpy as np
from jax import lax
from jax.experimental import pallas as pl
from jax.experimental.pallas import tpu as pltpu
from jax.sharding import PartitionSpec as P

NY = 64
NZ = 64
ITERS = 16
HALF = 32
FULL = 64
PACKED = HALF * HALF
MODES = 48
MARGIN = (MODES - HALF) // 2
PERIOD = 2 * (MODES + 1)
LANES = 128
FIELDS = 8
CLEARS = 16
MIB = 1024 * 1024
COUNT, PAIR, SLOT, SECOND, FIRST_A, FIRST_B, LAST_A, LAST_B, START_X, START_Y, START_Z, BLANK = range(12)
OWN_A, OWN_B, OWN_MEETS, OWN_X, OWN_Y, OWN_Z = range(12, 18)
FULL_ROWS = 24
BIG = 1 << 20

screening = 0.02
center_eig = 6.0 + screening
half_width = 6.0
sigma_one = center_eig / half_width


def spectrum():
    cosine = np.cos(np.pi * (np.arange(MODES) + 1) / (MODES + 1))
    lam = center_eig - 2.0 * (
        cosine[:, None, None] + cosine[None, :, None] + cosine[None, None, :]
    )
    solution_now, residue, ratio = np.zeros_like(lam), np.ones_like(lam), 1.0 / sigma_one
    update = residue / center_eig
    for _ in range(ITERS):
        solution_now = solution_now + update
        residue = residue - lam * update
        ratio_next = 1.0 / (2.0 * sigma_one - ratio)
        update = ratio_next * ratio * update + 2.0 * ratio_next / half_width * residue
        ratio = ratio_next
    table = -solution_now * (2.0 / (MODES + 1)) ** 3
    table = np.pad(table, ((0, 0), (0, 0), (0, LANES // 2 - MODES)))
    table = table.reshape(MODES // 16, 2, 8, MODES, LANES // 2).transpose(3, 2, 0, 1, 4)
    return table.reshape(MODES * 8, MODES // 16 * LANES).astype(np.float32)


def sine(mode, cell, start):
    place = (cell - start) & (HALF - 1)
    phase = ((mode + 1) * (place + MARGIN + 1)) % PERIOD
    return jnp.sin(phase.astype(jnp.float32) * np.float32(np.pi / (MODES + 1)))


def split(full):
    high = full.astype(jnp.bfloat16)
    return high, (full - high.astype(jnp.float32)).astype(jnp.bfloat16)


def halves(full):
    high = lax.reduce_precision(full, 8, 7)
    return high.astype(jnp.bfloat16), (full - high).astype(jnp.bfloat16)


def iotas(shape):
    return [lax.broadcasted_iota(jnp.int32, shape, d) for d in range(len(shape))]


def cell_y(q, g):
    return 2 * q + (g >> 1) + HALF // 2 * (g & 1)


def matrices(*starts):
    count = starts[0].shape[0]
    bx, by, bz = (start[:, None, None] for start in starts)

    def x_of(k, r):
        return sine(k, r, bx)

    def y_of(row, col):
        g, q = col >> 6, (col >> 3) & 7
        return jnp.where((row & 7) == (col & 7), sine(row >> 3, cell_y(q, g), by), 0.0)

    def z_of(row, col):
        same = ((row >> 7) == ((col >> 6) & 1)) & (((row >> 5) & 3) == (col >> 7))
        kz = col & 63
        return jnp.where(same & (kz < MODES), sine(kz, row & 31, bz), 0.0)

    out = []
    for of, rows, cols in ((x_of, MODES, HALF), (z_of, 256, 512), (y_of, MODES * 8, 256)):
        _, row, col = iotas((count, rows, cols))
        out += halves(of(row, col))
        _, row, col = iotas((count, cols, rows))
        out += halves(of(col, row))
    return out


def lane(shape):
    return lax.broadcasted_iota(jnp.int32, shape, len(shape) - 1)


def in_box(cell, start):
    return ((cell - start) & (FULL - 1)) < HALF


def fold(full, start_y, start_z):
    rows = full.shape[0]
    at = lane((rows, LANES))
    upper = (at >> 6) & 1
    in_z = in_box(at & 31, start_z)
    first = (at & 63) < 32
    picked = []
    for v in range(HALF // 2):
        low = full[:, v * LANES : (v + 1) * LANES]
        high = full[:, (v + HALF // 2) * LANES : (v + HALF // 2 + 1) * LANES]
        picked.append(jnp.where(in_box(2 * v + upper, start_y), low, high))
    out = []
    for q in range(8):
        a, b = picked[q], picked[q + 8]
        a = jnp.where(in_z, a, pltpu.roll(a, 96, 1))
        b = jnp.where(in_z, pltpu.roll(b, 32, 1), b)
        out.append(jnp.where(first, a, b))
    return out


def unfold(packed, start_y, start_z, row_mask):
    rows = packed.shape[0]
    at = lane((rows, LANES))
    upper = (at >> 6) & 1
    inside = in_box(at & 63, start_z) & row_mask
    first = (at & 63) < 32
    out = [None] * 32
    for v in range(16):
        piece = packed[:, (v % 8) * LANES : (v % 8 + 1) * LANES]
        if v < 8:
            wide = jnp.where(first, piece, pltpu.roll(piece, 32, 1))
        else:
            wide = jnp.where(first, pltpu.roll(piece, 96, 1), piece)
        wide = jnp.where(inside, wide, 0.0)
        in_y = in_box(2 * v + upper, start_y)
        out[v] = jnp.where(in_y, wide, 0.0)
        out[v + 16] = jnp.where(in_y, 0.0, wide)
    return out


def row_mask(first_row, rows, start_x):
    at = lax.broadcasted_iota(jnp.int32, (rows, LANES), 0)
    return in_box(at + first_row, start_x)


def mark_last(work, seen, terms, orb_dev):
    @pl.loop(0, terms)
    def _(n):
        i = terms - 1 - n
        for which, source in ((LAST_B, SECOND), (LAST_A, SLOT)):
            k = work[source, i]
            k = jnp.where(k < 0, orb_dev, k)
            work[which, i] = seen[k]
            seen[k] = 0


def pack_kernel(pair_dev, table_in, orbitals, out, work, table, held, packed, seen, sems, out_sems, table_sem):
    orb_dev, slab_rows, _ = orbitals.shape
    pairs = out.shape[0]
    base, first_row = lax.axis_index("orb") * orb_dev, lax.axis_index("slab") * slab_rows
    table_copy = pltpu.make_async_copy(table_in, table, table_sem)
    table_copy.start()
    packed[pairs] = jnp.zeros(packed.shape[1:], jnp.float32)
    for k in range(orb_dev + 1):
        seen[k] = 0
    table_copy.wait()

    def copy_of(index, slot):
        return pltpu.make_async_copy(orbitals.at[index], held.at[slot], sems.at[slot])

    def send(g, source):
        return pltpu.make_async_copy(packed.at[source], out.at[g], out_sems.at[g])

    def scan(g, carry):
        terms, blanks = carry
        row, off = g // pair_dev, (g % pair_dev) * FIELDS
        left, right = table[row, off] - base, table[row, off + 1] - base
        x = table[row, off + 2]
        meets = in_box(first_row, x) | in_box(first_row + slab_rows - 1, x)
        has_left = (left >= 0) & (left < orb_dev)
        has_right = (right >= 0) & (right < orb_dev)
        here = has_left | has_right
        live = here & meets
        both = has_left & has_right
        a = jnp.where(has_left, left, right)
        b = jnp.where(both, right, -1)
        work[PAIR, terms] = g
        work[SLOT, terms] = a
        work[SECOND, terms] = b
        work[START_X, terms] = x
        work[START_Y, terms] = table[row, off + 3]
        work[START_Z, terms] = table[row, off + 4]
        work[BLANK, blanks] = g

        @pl.when(live)
        def _():
            copy_of(a, 2 * terms).start()

            @pl.when(both)
            def _():
                copy_of(b, 2 * terms + 1).start()

        for which, k, used in ((FIRST_A, a, live), (FIRST_B, b, live & both)):
            k = jnp.where(used, k, orb_dev)
            old = seen[k]
            work[which, terms] = old
            seen[k] = 1
        terms = terms + jnp.where(live, 1, 0)
        return terms, blanks + jnp.where(here & jnp.logical_not(meets), 1, 0)

    zero = jnp.int32(0)
    terms, blanks = lax.fori_loop(0, pairs, scan, (zero, zero), unroll=4)
    work[COUNT, 0] = terms
    work[COUNT, 1] = first_row

    @pl.loop(0, blanks)
    def _(i):
        send(work[BLANK, i], pairs).start()

    mark_last(work, seen, terms, orb_dev)

    @pl.loop(0, terms)
    def _(i):
        g = work[PAIR, i]

        def put(full):
            mask = row_mask(first_row, slab_rows, work[START_X, i])
            for q, piece in enumerate(fold(full, work[START_Y, i], work[START_Z, i])):
                packed[g, :, q * LANES : (q + 1) * LANES] = jnp.where(mask, piece, 0.0)
            send(g, g).start()

        copy_of(work[SLOT, i], 2 * i).wait()

        @pl.when(work[SECOND, i] >= 0)
        def _():
            copy_of(work[SECOND, i], 2 * i + 1).wait()
            put(held[2 * i] * held[2 * i + 1])

        @pl.when(work[SECOND, i] < 0)
        def _():
            put(held[2 * i])

    @pl.loop(0, terms)
    def _(i):
        send(work[PAIR, i], work[PAIR, i]).wait()

    @pl.loop(0, blanks)
    def _(i):
        send(work[BLANK, i], pairs).wait()


def clear_kernel(after, out, done, blank, sems):
    done[...] = jnp.full(done.shape, after[0, 0], jnp.int32)
    count = blank.shape[0]
    blank[...] = jnp.zeros(blank.shape, jnp.float32)
    copies = [
        pltpu.make_async_copy(blank, out.at[c * count : (c + 1) * count], sems.at[c])
        for c in range(CLEARS)
    ]
    for c in copies:
        c.start()
    for c in copies:
        c.wait()


def dot3(a, b):
    def dot(left, right):
        return jnp.dot(left, right, preferred_element_type=jnp.float32)

    return dot(a[0], b[0]) + (dot(a[0], b[1]) + dot(a[1], b[0]))


def tile(full, row, col):
    return full[row * 8 : row * 8 + 8, col * LANES : (col + 1) * LANES]


def blocks(rows):
    return jnp.concatenate([jnp.concatenate(r, axis=1) for r in rows], axis=0)


def potential_of(density, x, xt, z, zt, y, yt, weights):
    pairs_x = MODES // 16
    u = dot3(x, split(density))
    u = blocks(
        [[tile(u, 2 * tp + par, q) for par in range(2)] for tp in range(pairs_x) for q in range(8)]
    )
    u = dot3(split(u), z)
    u = blocks(
        [[tile(u, tp * 8 + q, g) for tp in range(pairs_x)] for g in range(4) for q in range(8)]
    )
    u = dot3(y, split(u)) * weights
    u = dot3(yt, split(u))
    u = blocks(
        [[tile(u, g * 8 + q, tp) for g in range(4)] for tp in range(pairs_x) for q in range(8)]
    )
    u = dot3(split(u), zt)
    u = blocks(
        [[tile(u, tp * 8 + q, par) for q in range(8)] for tp in range(pairs_x) for par in range(2)]
    )
    return dot3(xt, split(u))


def solve_kernel(orb_dev, own, received, cleared, *refs):
    del cleared
    mats, weights, out = refs[:12], *refs[12:]
    n_slab, _, pair_dev, rows, _ = received.shape
    half = n_slab // 2
    for i in range(pair_dev):
        plane = [own[i, side] // orb_dev for side in range(2)]
        sides = [
            jnp.concatenate(
                [received[s, at, i] + received[s + half, at, i] for s in range(half)], axis=0
            )
            for at in plane
        ]
        together = plane[0] == plane[1]
        density = jnp.where(together, sides[0], sides[0] * sides[1])
        m = [(mats[k][i], mats[k + 1][i]) for k in range(0, 12, 2)]
        potential = potential_of(density, *m, weights[...])
        for side in range(2):
            term = jnp.where(together, potential, potential * sides[1 - side])
            for s in range(half):
                part = term[s * rows : (s + 1) * rows]
                out[s, plane[side], i] = part
                out[s + half, plane[side], i] = part


def place_kernel(work, orbitals, returned, zeros, out, held, acc, sems, out_sems):
    del zeros
    place_terms(work, orbitals, lambda at: returned[at], out, held, acc, sems, out_sems)


def place_terms(work, orbitals, fetch, out, held, acc, sems, out_sems):
    _, slab_rows, _ = orbitals.shape
    terms, first_row = work[COUNT, 0], work[COUNT, 1]

    def factors(i):
        return [
            pltpu.make_async_copy(
                orbitals.at[work[which, i]], held.at[2 * i + n], sems.at[2 * i + n]
            )
            for n, which in enumerate((SLOT, SECOND))
        ]

    def copy_out(k):
        return pltpu.make_async_copy(acc.at[k], out.at[k], out_sems.at[k])

    @pl.loop(0, terms)
    def _(i):
        @pl.when(work[SECOND, i] >= 0)
        def _():
            for c in factors(i):
                c.start()

    @pl.loop(0, terms)
    def _(i):
        a, b = work[SLOT, i], work[SECOND, i]
        mask = row_mask(first_row, slab_rows, work[START_X, i])
        pieces = unfold(fetch(work[PAIR, i]), work[START_Y, i], work[START_Z, i], mask)

        def add(k, later, last, slot):
            def term(v):
                if slot is None:
                    return pieces[v]
                return pieces[v] * held[slot, :, v * LANES : (v + 1) * LANES]

            @pl.when(later == 0)
            def _():
                for v in range(len(pieces)):
                    acc[k, :, v * LANES : (v + 1) * LANES] = term(v)

            @pl.when(later != 0)
            def _():
                for v in range(len(pieces)):
                    acc[k, :, v * LANES : (v + 1) * LANES] += term(v)

            @pl.when(last != 0)
            def _():
                copy_out(k).start()

        @pl.when(b >= 0)
        def _():
            for c in factors(i):
                c.wait()
            add(a, work[FIRST_A, i], work[LAST_A, i], 2 * i + 1)
            add(b, work[FIRST_B, i], work[LAST_B, i], 2 * i)

        @pl.when(b < 0)
        def _():
            add(a, work[FIRST_A, i], work[LAST_A, i], None)

    @pl.loop(0, terms)
    def _(i):
        @pl.when(work[LAST_A, i] != 0)
        def _():
            copy_out(work[SLOT, i]).wait()

        @pl.when((work[SECOND, i] >= 0) & (work[LAST_B, i] != 0))
        def _():
            copy_out(work[SECOND, i]).wait()


def quotient(value, by):
    return value >> (by.bit_length() - 1) if by & (by - 1) == 0 else value // by


def pick(begins, parts, index, act):
    for begin, part in zip(begins, parts, strict=True):
        inside = (index >= begin) & (index < begin + part.shape[0])
        pl.when(inside)(lambda part=part, begin=begin: act(part, index - begin))


def slab_fields(n_slab, slab_rows):
    if n_slab > 8:
        return np.ones((FULL,), np.int32), 0
    bits = np.zeros((FULL,), np.int64)
    for x in range(FULL):
        for slab in range(n_slab):
            ends = (slab * slab_rows, (slab + 1) * slab_rows - 1)
            if any((e - x) % FULL < HALF for e in ends):
                bits[x] += 1 << (4 * slab)
    return bits.astype(np.uint32).view(np.int32), 4


def crossing_slots(cap, n_orb):
    near = max(cap * 3 // 4, 1)
    far = max(cap * 3 // 8, 1)
    step = max(cap // 8, 1)
    return [(near, 0, 0) if d == 1 else (far, step, step) for d in range(1, n_orb)]


def route_kernel(
    pair_dev, n_orb, width, table_in, fields, orbitals, *refs
):
    *sends, own, work, table, held, seen, load, pieces, crossing, chosen, sems, table_sem = refs
    orb_dev, slab_rows, _ = orbitals.shape
    pairs = table.shape[0] * pair_dev
    cap = own.shape[0]
    spans = crossing_slots(cap, n_orb)
    slots = [sum(span) for span in spans]
    begins = [0] + [cap + sum(slots[:d]) for d in range(n_orb - 1)]
    fewer = [d for d, span in enumerate(spans) if span[1]]
    begins += [begins[d + 1] for d in fewer] * (len(spans[0]) - 1)
    me = lax.axis_index("orb")
    slab = lax.axis_index("slab")
    base, first_row = me * orb_dev, slab * slab_rows
    table_copy = pltpu.make_async_copy(table_in, table, table_sem)
    table_copy.start()
    for k in range(orb_dev + 1):
        seen[k] = 0
    for k in range(n_orb):
        load[k] = 0
    for k in range(n_orb * n_orb):
        pieces[k] = 0
        crossing[k] = 0
    table_copy.wait()

    def copy_of(index, slot):
        return pltpu.make_async_copy(orbitals.at[index], held.at[slot], sems.at[slot])

    def scan(g, terms):
        row, off = g // pair_dev, (g % pair_dev) * FIELDS
        left, right = table[row, off], table[row, off + 1]
        x, y, z = (table[row, off + 2 + d] for d in range(3))
        a, b = quotient(left, orb_dev), quotient(right, orb_dev)
        weight = jnp.where((a ^ b) == 1, 0, 2)
        load_a, load_b = load[a], load[b]
        cost_a = jnp.where(load_a < cap, load_a + weight * pieces[b * n_orb + a], BIG)
        cost_b = jnp.where(load_b < cap, load_b + weight * pieces[a * n_orb + b], BIG)
        chosen[0] = jnp.where(cost_a <= cost_b, a, b)

        @pl.when((load_a >= cap) & (load_b >= cap))
        def _():
            least = jnp.int32(0)
            for o in range(1, n_orb):
                least = jnp.where(load[o] < load[least], o, least)
            chosen[0] = least

        k = chosen[0]
        j = load[k]
        load[k] = j + 1
        here = fields[x]
        meets = in_box(first_row, x) | in_box(first_row + slab_rows - 1, x)

        def cross(o, used):
            at = o * n_orb + k
            taken = crossing[at]
            crossing[at] = taken + jnp.where(used, here, 0)
            pieces[at] = pieces[at] + jnp.where(used, 1, 0)
            count = (taken >> (width * slab)) & 15 if width else taken
            d = o ^ k
            begin, room = jnp.int32(cap), jnp.int32(slots[0])
            for n in range(1, len(slots)):
                begin = jnp.where(d == n + 1, cap + sum(slots[:n]), begin)
                room = jnp.where(d == n + 1, slots[n], room)
            return begin + jnp.minimum(count, room - 1)

        away_a = a != k
        away_b = (b != k) & (a != b)
        at_a = cross(a, away_a)
        at_b = cross(b, away_b)
        mine = k == me

        @pl.when(mine)
        def _():
            both_away = away_a & away_b
            work[OWN_A, j] = jnp.where(both_away | (away_a & (a == b)), at_a, j)
            work[OWN_B, j] = jnp.where(away_b, at_b, jnp.where(away_a & (a != b), at_a, -1))
            work[OWN_MEETS, j] = jnp.where(meets, 1, 0)
            work[OWN_X, j] = x
            work[OWN_Y, j] = y
            work[OWN_Z, j] = z

        has_left, has_right = a == me, b == me
        live = (has_left | has_right) & meets
        both = has_left & has_right
        first = jnp.where(has_left, left, right) - base
        second = jnp.where(both, right - base, -1)
        work[PAIR, terms] = jnp.where(mine, j, jnp.where(has_left, at_a, at_b))
        work[SLOT, terms] = first
        work[SECOND, terms] = second
        work[START_X, terms] = x
        work[START_Y, terms] = y
        work[START_Z, terms] = z

        @pl.when(live)
        def _():
            copy_of(first, 2 * terms).start()

            @pl.when(both)
            def _():
                copy_of(second, 2 * terms + 1).start()

        for which, index, used in ((FIRST_A, first, live), (FIRST_B, second, live & both)):
            index = jnp.where(used, index, orb_dev)
            work[which, terms] = seen[index]
            seen[index] = 1
        return terms + jnp.where(live, 1, 0)

    terms = lax.fori_loop(0, pairs, scan, jnp.int32(0), unroll=2)
    level = jnp.int32(0)
    for o in range(n_orb):
        for k in range(n_orb):
            if o != k:
                span, count = spans[(o ^ k) - 1], crossing[o * n_orb + k]
                for f in range(8 if width else 1):
                    held_here = (count >> (width * f)) & 15 if width else count
                    for at in range(len(span)):
                        room = sum(span[: at + 1])
                        level = jnp.maximum(level, jnp.where(held_here > room, at + 1, 0))
    work[COUNT, 0] = terms
    work[COUNT, 1] = first_row
    work[COUNT, 2] = level
    mark_last(work, seen, terms, orb_dev)

    @pl.loop(0, terms)
    def _(i):
        def put(full):
            mask = row_mask(first_row, slab_rows, work[START_X, i])
            folded = [
                jnp.where(mask, piece, 0.0)
                for piece in fold(full, work[START_Y, i], work[START_Z, i])
            ]

            def store(ref, n):
                for q, piece in enumerate(folded):
                    ref[n, :, q * LANES : (q + 1) * LANES] = piece

            pick(begins, [own, *sends], work[PAIR, i], store)

        copy_of(work[SLOT, i], 2 * i).wait()

        @pl.when(work[SECOND, i] >= 0)
        def _():
            copy_of(work[SECOND, i], 2 * i + 1).wait()
            put(held[2 * i] * held[2 * i + 1])

        @pl.when(work[SECOND, i] < 0)
        def _():
            put(held[2 * i])


def density_kernel(begins, work, *refs):
    *parts, out, start_y, side = refs
    pair_dev = start_y.shape[1]
    for i in range(pair_dev):
        start_y[0, i] = work[OWN_Y, lax.axis_index("slab") * pair_dev + i]

    def load(ref, n):
        side[...] = ref[n]

    @pl.loop(0, out.shape[0], unroll=2)
    def _(j):
        a, b = work[OWN_A, j], work[OWN_B, j]
        meets = work[OWN_MEETS, j] != 0

        @pl.when(meets)
        def _():
            pick(begins, parts, a, load)

        def both(ref, n):
            out[j] = side[...] * ref[n]

        @pl.when(meets & (b >= 0))
        def _():
            pick(begins, parts, b, both)

        @pl.when(meets & (b < 0))
        def _():
            out[j] = side[...]

        @pl.when(jnp.logical_not(meets))
        def _():
            out[j] = jnp.zeros(out.shape[1:], jnp.float32)


def plane_solve_kernel(received, *refs):
    mats, weights, out = refs[:12], *refs[12:]
    n_slab, pair_dev, rows, _ = received.shape
    half = n_slab // 2
    for i in range(pair_dev):
        density = jnp.concatenate(
            [received[s, i] + received[s + half, i] for s in range(half)], axis=0
        )
        m = [(mats[k][i], mats[k + 1][i]) for k in range(0, 12, 2)]
        potential = potential_of(density, *m, weights[...])
        for s in range(half):
            part = potential[s * rows : (s + 1) * rows]
            out[s, i] = part
            out[s + half, i] = part


def term_kernel(begins, work, potential, *refs):
    count = (len(refs) - 2) // 2
    parts, outs = refs[:count], refs[count : 2 * count]
    after, term = refs[-2:]
    after[0, 0] = work[COUNT, 0]

    def store(ref, n):
        ref[n] = term[...]

    @pl.loop(0, potential.shape[0], unroll=2)
    def _(j):
        a, b = work[OWN_A, j], work[OWN_B, j]
        meets = work[OWN_MEETS, j] != 0

        def times(ref, n):
            term[...] = potential[j] * ref[n]

        @pl.when(meets & (b >= 0))
        def _():
            for source, target in ((a, b), (b, a)):
                pick(begins, parts, source, times)
                pick(begins, outs, target, store)

        @pl.when(meets & (b < 0))
        def _():
            term[...] = potential[j]
            pick(begins, outs, a, store)


def plane_place_kernel(begins, work, orbitals, zeros, *refs):
    del zeros
    *parts, out, held, acc, term, sems, out_sems = refs

    def load(ref, n):
        term[...] = ref[n]

    def fetch(at):
        pick(begins, parts, at, load)
        return term[...]

    place_terms(work, orbitals, fetch, out, held, acc, sems, out_sems)


def body(orbitals, pair_list, box_start):
    n_slab = lax.axis_size("slab")
    n_orb = lax.axis_size("orb")
    axes = ("slab", "orb")
    orb_dev, slab_rows, cells = orbitals.shape
    pair_dev = pair_list.shape[0]
    devices = n_slab * n_orb
    pairs = devices * pair_dev

    smem = pl.BlockSpec(memory_space=pltpu.SMEM)
    vmem = pl.BlockSpec(memory_space=pltpu.VMEM)
    free = pl.BlockSpec(memory_space=pl.ANY)
    hbm = pl.BlockSpec(memory_space=pltpu.HBM)
    slots = (pairs, slab_rows, PACKED)
    held = pltpu.VMEM((2 * pairs, slab_rows, cells), jnp.float32)

    def grant(mib):
        return pltpu.CompilerParams(vmem_limit_bytes=mib * MIB)

    width = -(-pair_dev * FIELDS // LANES) * LANES
    row = jnp.concatenate([pair_list, box_start], axis=1)
    row = jnp.pad(row, ((0, 0), (0, FIELDS - row.shape[1]))).reshape(1, pair_dev * FIELDS)
    row = jnp.pad(row, ((0, 0), (0, width - row.shape[1])))
    table = lax.all_to_all(
        jnp.broadcast_to(row, (devices, width)), axes, split_axis=0, concat_axis=0, tiled=True
    )

    cap = pairs // n_orb
    spans = crossing_slots(cap, n_orb)
    rooms = [sum(span) for span in spans]
    begins = [0] + [cap + sum(rooms[:d]) for d in range(n_orb - 1)]
    fields, field_bits = slab_fields(n_slab, slab_rows)
    lists = jax.ShapeDtypeStruct((FULL_ROWS, -(-(2 * pairs + 1) // LANES) * LANES), jnp.int32)
    one_plane = jax.ShapeDtypeStruct((cap, slab_rows, PACKED), jnp.float32)

    def crossed(level):
        return [
            jax.ShapeDtypeStruct((sum(span[: level + 1]), slab_rows, PACKED), jnp.float32)
            for span in spans
        ]

    fewer = [d for d, span in enumerate(spans) if span[1]]
    top = len(spans[0]) - 1
    leaving = crossed(top) + [crossed(level)[d] for level in range(top) for d in fewer]
    one_slot = pltpu.VMEM((slab_rows, PACKED), jnp.float32)

    def cross(parts):
        return [
            lax.ppermute(part, "orb", [(o, o ^ (n + 1)) for o in range(n_orb)])
            for n, part in enumerate(parts)
        ]

    def clear(work):
        return pl.pallas_call(
            clear_kernel,
            out_shape=[
                jax.ShapeDtypeStruct(orbitals.shape, jnp.float32),
                jax.ShapeDtypeStruct((8, LANES), jnp.int32),
            ],
            in_specs=[smem],
            out_specs=[hbm, vmem],
            scratch_shapes=[
                pltpu.VMEM((orb_dev // CLEARS, slab_rows, cells), jnp.float32),
                pltpu.SemaphoreType.DMA((CLEARS,)),
            ],
            compiler_params=grant(16),
            cost_estimate=pl.CostEstimate(
                flops=0, bytes_accessed=orbitals.size * 4, transcendentals=0
            ),
            name="clear",
        )(work)

    *sends, own_pieces, work = pl.pallas_call(
        functools.partial(route_kernel, pair_dev, n_orb, field_bits),
        out_shape=[*leaving, one_plane, lists],
        in_specs=[free, smem, hbm],
        out_specs=[vmem] * (len(leaving) + 1) + [smem],
        scratch_shapes=[
            pltpu.SMEM((devices, width), jnp.int32),
            held,
            pltpu.SMEM((orb_dev + 1,), jnp.int32),
            pltpu.SMEM((n_orb,), jnp.int32),
            pltpu.SMEM((n_orb * n_orb,), jnp.int32),
            pltpu.SMEM((n_orb * n_orb,), jnp.int32),
            pltpu.SMEM((1,), jnp.int32),
            pltpu.SemaphoreType.DMA((2 * pairs,)),
            pltpu.SemaphoreType.DMA,
        ],
        compiler_params=grant(56),
        name="route",
    )(table, jnp.asarray(fields), orbitals)

    def in_planes(level, table, orbitals, box_start, work, own_pieces, *sends):
        del table, box_start
        sends, short = list(sends[: n_orb - 1]), sends[n_orb - 1 :]
        if level < top:
            for d, part in zip(fewer, short[level * len(fewer) :]):
                sends[d] = part
        arrived = cross(sends)
        starts = lax.dynamic_slice(
            work, (OWN_X, lax.axis_index("slab") * pair_dev), (3, pair_dev)
        )
        density, start_y = pl.pallas_call(
            functools.partial(density_kernel, begins),
            out_shape=[one_plane, jax.ShapeDtypeStruct((1, pair_dev), jnp.int32)],
            in_specs=[smem] + [vmem] * n_orb,
            out_specs=[vmem, smem],
            scratch_shapes=[one_slot],
            compiler_params=grant(8),
            name="density",
        )(work, own_pieces, *arrived)
        mats = matrices(starts[0], start_y[0], starts[2])
        received = lax.all_to_all(density, "slab", split_axis=0, concat_axis=0, tiled=True)
        by_slab = (n_slab, pair_dev, slab_rows, PACKED)
        solved = pl.pallas_call(
            plane_solve_kernel,
            out_shape=jax.ShapeDtypeStruct(by_slab, jnp.float32),
            in_specs=[vmem] * 14,
            out_specs=vmem,
            compiler_params=grant(16),
            name="solve",
        )(received.reshape(by_slab), *mats, jnp.asarray(spectrum()))
        potential = lax.all_to_all(
            solved.reshape(one_plane.shape), "slab", split_axis=0, concat_axis=0, tiled=True
        )
        own_terms, *sends, after = pl.pallas_call(
            functools.partial(term_kernel, begins),
            out_shape=[one_plane, *crossed(level), jax.ShapeDtypeStruct((1, 1), jnp.int32)],
            in_specs=[smem, vmem] + [vmem] * n_orb,
            out_specs=[vmem] * n_orb + [smem],
            scratch_shapes=[one_slot],
            compiler_params=grant(8),
            name="terms",
        )(work, potential, own_pieces, *arrived)
        arrived = cross(sends)
        zeros, _ = clear(after)
        return pl.pallas_call(
            functools.partial(plane_place_kernel, begins),
            out_shape=jax.ShapeDtypeStruct(orbitals.shape, jnp.float32),
            in_specs=[smem, hbm, hbm] + [vmem] * n_orb,
            out_specs=hbm,
            scratch_shapes=[
                held,
                pltpu.VMEM(orbitals.shape, jnp.float32),
                one_slot,
                pltpu.SemaphoreType.DMA((2 * pairs,)),
                pltpu.SemaphoreType.DMA((orb_dev,)),
            ],
            input_output_aliases={2: 0},
            compiler_params=grant(52),
            name="place",
        )(work, orbitals, zeros, own_terms, *arrived)

    def direct(table, orbitals, box_start, *unused):
        del unused
        outgoing, work = pl.pallas_call(
            functools.partial(pack_kernel, pair_dev),
            out_shape=[
                jax.ShapeDtypeStruct(slots, jnp.float32),
                lists,
            ],
            in_specs=[free, hbm],
            out_specs=[hbm, smem],
            scratch_shapes=[
                pltpu.SMEM((devices, width), jnp.int32),
                held,
                pltpu.VMEM((pairs + 1, slab_rows, PACKED), jnp.float32),
                pltpu.SMEM((orb_dev + 1,), jnp.int32),
                pltpu.SemaphoreType.DMA((2 * pairs,)),
                pltpu.SemaphoreType.DMA((pairs,)),
                pltpu.SemaphoreType.DMA,
            ],
            compiler_params=grant(56),
            name="pack",
        )(table, orbitals)
        received = lax.all_to_all(outgoing, axes, split_axis=0, concat_axis=0, tiled=True)

        zeros, cleared = clear(work)

        solved = pl.pallas_call(
            functools.partial(solve_kernel, orb_dev),
            out_shape=jax.ShapeDtypeStruct((n_slab, n_orb, pair_dev, slab_rows, PACKED), jnp.float32),
            in_specs=[smem] + [vmem] * 15,
            out_specs=vmem,
            compiler_params=grant(16),
            name="solve",
        )(
            pair_list,
            received.reshape(n_slab, n_orb, pair_dev, slab_rows, PACKED),
            cleared,
            *matrices(*box_start.T),
            jnp.asarray(spectrum()),
        )
        returned = lax.all_to_all(solved.reshape(slots), axes, split_axis=0, concat_axis=0, tiled=True)

        return pl.pallas_call(
            place_kernel,
            out_shape=jax.ShapeDtypeStruct(orbitals.shape, jnp.float32),
            in_specs=[smem, hbm, vmem, hbm],
            out_specs=hbm,
            scratch_shapes=[
                held,
                pltpu.VMEM(orbitals.shape, jnp.float32),
                pltpu.SemaphoreType.DMA((2 * pairs,)),
                pltpu.SemaphoreType.DMA((orb_dev,)),
            ],
            input_output_aliases={3: 0},
            compiler_params=grant(52),
            name="place",
        )(work, orbitals, returned, zeros)

    return lax.switch(
        work[COUNT, 2],
        [*(functools.partial(in_planes, level) for level in range(top + 1)), direct],
        table,
        orbitals,
        box_start,
        work,
        own_pieces,
        *sends,
    )


def solution(mesh):
    return jax.shard_map(
        body,
        mesh=mesh,
        in_specs=(P("orb", "slab", None), P(("slab", "orb"), None), P(("slab", "orb"), None)),
        out_specs=P("orb", "slab", None),
        check_vma=False,
    )
```
